32 devices in a mesh: row: 4 (over x, core), col: 8 (over z, y).
Axes of the slice: x: 2, y: 2, z: 4, core: 2. Of those that a mesh axis runs over, the one named last changes fastest.
Arguments:
- front_blocks: float32 [32, 512, 16, 1024], P(None, 'row', None, 'col'), may hold values from -2.5 to 10.5, as said below
- child_updates: bfloat16 [2, 24, 512, 12, 1024], P(None, None, 'row', None, 'col'), may hold values from -0.2 to 2.2, as said below
- child_map: int32 [2, 96], replicated, may hold values from 0 to 127, as said below
Outputs:
- factored: float32 [32, 512, 16, 1024], P(None, 'row', None, 'col')
The draws below stay inside these ranges and needn't reach their ends.
Inputs may be any that keep to these rules, and one draw needn't show every extreme that they name: `child_map`: for each child, block a * 8 + j (0 <= j < 8) lands in front block h_a * 8 + ((s_a - j) mod 8), with 12 distinct h_a below 16 and s_a = (s + q_a) mod 8, q a permutation of 0 .. 11. Hence along col one device sends at most 2 of a child's column blocks to one device, along row at most 6 of its row blocks, and both bounds are reached in every draw. `front_blocks`: symmetric positive definite. `child_updates`: each child update is symmetric.
All inputs are finite; a program needn't handle non-finite values.
Results may differ from the reference program's by a relative error of at most 0.0003.
Values may be sent and summed in bfloat16 or wider, within the bound.
No kernel may reach another device: no remote copies, remote signals or barrier semaphores. Data moves between devices by JAX's collectives and lax.ppermute only.
A program may use at most 256 MiB of HBM per device.

```python
import math
import jax
import jax.numpy as jnp
from jax import lax

F = 16384
C = 12288
BLK = 128
PW = 256
PANELS = 2
PROW = 4
PCOL = 8
CB = 96
SROW = 32
SCOL = 16
KROW = 24
KCOL = 12
PD = 512


def symmetric_part(key, order, diag_low, diag_high):
    noise_key, diag_key = jax.random.split(key)
    noise = jnp.clip(jax.random.normal(noise_key, (order, order), jnp.float32), -4.0, 4.0)
    diag_values = jax.random.uniform(diag_key, (order,), jnp.float32, diag_low, diag_high)
    scale = 0.4 / math.sqrt(order)
    matrix = (noise + noise.T) * (scale / math.sqrt(2.0))
    positions = jnp.arange(order)
    return matrix.at[positions, positions].add(diag_values)


def draw_front_blocks(key, part):
    inner = max(F // 16, 128)
    factor_key, diag_key = jax.random.split(key)
    coupling = jnp.clip(jax.random.normal(factor_key, (F, inner), jnp.float32), -4.0, 4.0)
    diag_values = jax.random.uniform(diag_key, (F,), jnp.float32, 1.0, 3.0)
    coupling = coupling * (2.0 / math.sqrt(inner))
    gram = jnp.dot(coupling, coupling.T, precision=lax.Precision.HIGHEST, preferred_element_type=jnp.float32)
    gram = 0.5 * (gram + gram.T)
    positions = jnp.arange(F)
    matrix = gram.at[positions, positions].add(diag_values)
    return matrix.reshape(SROW, BLK * PROW, SCOL, BLK * PCOL)


def draw_child_updates(key, part):
    stacked = jnp.stack([symmetric_part(jax.random.fold_in(key, 11 + child_no), C, 1.0, 2.0) for child_no in range(2)])
    return stacked.reshape(2, KROW, BLK * PROW, KCOL, BLK * PCOL).astype(jnp.bfloat16)


def draw_child_map(key, part):
    rows_out = []
    for child_no in range(2):
        child_key = jax.random.fold_in(key, 101 + child_no)
        home_key, order_key, base_key = jax.random.split(child_key, 3)
        home_list = jax.random.permutation(home_key, SCOL)[:KCOL].astype(jnp.int32)
        order_list = jax.random.permutation(order_key, KCOL).astype(jnp.int32)
        base_shift = jax.random.randint(base_key, (), 0, PCOL, dtype=jnp.int32)
        shifts = (base_shift + order_list) % PCOL
        lanes = jnp.arange(PCOL, dtype=jnp.int32)
        block_list = home_list[:, None] * PCOL + (shifts[:, None] - lanes[None, :] + PCOL) % PCOL
        rows_out.append(block_list.reshape(CB))
    return jnp.stack(rows_out).astype(jnp.int32)


def setup_inputs(seed: int = 0) -> dict:
    seeds = jax.random.split(jax.random.key(seed), 4)
    front_blocks = draw_front_blocks(jax.random.fold_in(seeds[3], 71), 0)
    child_updates = draw_child_updates(jax.random.fold_in(seeds[3], 71), 0)
    child_map = draw_child_map(jax.random.fold_in(seeds[3], 71), 0)
    return {"front_blocks": front_blocks, "child_updates": child_updates, "child_map": child_map}


def reference(front_blocks, child_updates, child_map):
    matrix = front_blocks.reshape(F, F)
    offsets = jnp.arange(BLK, dtype=jnp.int32)
    children = child_updates.reshape(2, C, C)
    for child_no in range(2):
        index_list = (child_map[child_no][:, None] * BLK + offsets[None, :]).reshape(C).astype(jnp.int32)
        matrix = matrix.at[index_list[:, None], index_list[None, :]].add(children[child_no].astype(jnp.float32))
    row_ids = jnp.arange(F, dtype=jnp.int32)
    factors = []
    for panel_no in range(PANELS):
        first_col = panel_no * PW
        finish = first_col + PW
        factor = jnp.linalg.cholesky(matrix[first_col:finish, first_col:finish])
        solved = lax.linalg.triangular_solve(factor, matrix[:, first_col:finish], left_side=False, lower=True, transpose_a=True)
        lower_part = jnp.where(row_ids[:, None] >= finish, solved, jnp.zeros_like(solved))
        lower_part = lower_part.at[first_col:finish].set(factor)
        matrix = matrix - jnp.dot(lower_part.astype(jnp.float32), lower_part.T.astype(jnp.float32), precision=lax.Precision.HIGHEST, preferred_element_type=jnp.float32)
        factors.append(lower_part)
    result = matrix.at[:, :PD].set(jnp.concatenate(factors, axis=1))
    result = result.at[:PD, PD:].set(jnp.zeros((PD, F - PD), result.dtype))
    return result.reshape(SROW, BLK * PROW, SCOL, BLK * PCOL)
```

```python
import functools

import jax
import jax.numpy as jnp
from jax import lax
from jax.experimental import pallas as pl
from jax.experimental.pallas import tpu as pltpu
from jax.sharding import Mesh, PartitionSpec as P

PD = 512
TILE = 128
PT = PD // TILE
COL = ("half", "lane")
AXES = ("row",) + COL
VMEM_LIMIT = 48 * 1024 * 1024


class Plan:
    def __init__(self, rows, lanes, groups, homes):
        self.R, self.L, self.G = rows, lanes, groups
        self.cap_r = -(-groups // rows)
        self.cap_l = -(-groups // lanes)
        self.shift = 0
        self.home = self.shift + 2 * groups
        self.by_class = self.home + 2 * groups
        self.by_shift = self.by_class + 2 * rows * self.cap_r
        self.first = self.by_shift + 2 * lanes * self.cap_l
        self.homes = homes
        self.at_home = self.first + 2
        self.rank = self.at_home + 2 * homes
        self.rho = self.rank + 2 * groups
        self.kap = self.rho + 1

    def get_shift(self, tab, i, a):
        return tab[self.shift + i * self.G + a]

    def get_home(self, tab, i, a):
        return tab[self.home + i * self.G + a]

    def class_entry(self, tab, i, m, t):
        return tab[self.by_class + (i * self.R + m) * self.cap_r + t]

    def shift_entry(self, tab, i, s, t):
        return tab[self.by_shift + (i * self.L + s) * self.cap_l + t]

    def place(self, tab):
        kap = tab[self.kap]
        return tab[self.rho], kap // self.R, lax.rem(kap, self.R)


def make_table(plan, child_map):
    R, L, G = plan.R, plan.L, plan.G
    lead = child_map.reshape(2, G, L)[:, :, 0]
    shift, home = lead % L, lead // L
    ids = jnp.arange(G, dtype=jnp.int32)
    before = ids[None, :] < ids[:, None]

    def inverse(keys, count, capacity):
        rank = jnp.sum((keys[:, :, None] == keys[:, None, :]) & before[None], axis=2)
        hit = (keys[:, None, None, :] == jnp.arange(count)[None, :, None, None]) & (
            rank[:, None, None, :] == jnp.arange(capacity)[None, None, :, None]
        )
        return jnp.max(jnp.where(hit, ids[None, None, None, :], -1), axis=3)

    at_home = inverse(home, plan.homes, 1)
    same = (shift % R)[:, :, None] == (shift % R)[:, None, :]
    rank = jnp.sum(same & before[None], axis=2)
    parts = [shift, home, inverse(shift % R, R, plan.cap_r), inverse(shift, L, plan.cap_l), at_home[:, 0], at_home, rank]
    here = [lax.axis_index("row"), lax.axis_index(COL)]
    return jnp.concatenate(
        [p.reshape(-1).astype(jnp.int32) for p in parts] + [h.reshape(1).astype(jnp.int32) for h in here]
    )


def modr(value, n):
    return lax.rem(value + 2 * n, n)


def pack_near(plan, table, updates):
    R, L = plan.R, plan.L
    slots = updates.shape[2]

    def body(tab, x_ref, out):
        i = pl.program_id(0)
        kap = tab[plan.kap]
        for k in range(L):
            for t in range(plan.cap_l):
                b = plan.shift_entry(tab, i, lax.rem(kap + k, L), t)

                @pl.when(b >= 0)
                def _(k=k, t=t, b=b):
                    out[0, k // R, k % R, 0, 0, t] = x_ref[0, 0, b]

    def in_map(i, r, t, tab):
        rho, h, _ = plan.place(tab)
        return (i, 2 * jnp.maximum(plan.class_entry(tab, i, lax.rem(r + rho, R), t), 0) + h, 0, 0, 0)

    shape = (R, 2, R, 2, plan.cap_r, plan.cap_l, TILE, TILE)
    return pl.pallas_call(
        body,
        grid_spec=pltpu.PrefetchScalarGridSpec(
            num_scalar_prefetch=1,
            grid=(2, R, plan.cap_r),
            in_specs=[pl.BlockSpec((1, 1, slots, TILE, TILE), in_map)],
            out_specs=pl.BlockSpec(
                (1, 2, R, 1, 1, plan.cap_l, TILE, TILE), lambda i, r, t, tab: (r, 0, 0, i, t, 0, 0, 0)
            ),
        ),
        out_shape=jax.ShapeDtypeStruct(shape, jnp.bfloat16),
        compiler_params=pltpu.CompilerParams(vmem_limit_bytes=VMEM_LIMIT),
        name="pack_near",
    )(table, updates)


def pack_far(plan, table, updates):
    R, L = plan.R, plan.L
    slots = updates.shape[2]
    shape = jax.ShapeDtypeStruct((R, R, 2, 2, plan.cap_r, plan.cap_l, TILE, TILE), jnp.bfloat16)
    in_block = (1, 1, slots, TILE, TILE)

    def direct(tab, x_ref, out):
        i = pl.program_id(0)
        kap = tab[plan.kap]
        h = kap // R
        for k in range(R):
            for t in range(plan.cap_l):
                b = plan.shift_entry(tab, i, lax.rem(kap + h * R + k, L), t)

                @pl.when(b >= 0)
                def _(k=k, t=t, b=b):
                    out[0, k, 0, 0, 0, t] = x_ref[0, 0, b]

    def direct_map(i, r, t, tab):
        rho, h, _ = plan.place(tab)
        return (i, 2 * jnp.maximum(plan.class_entry(tab, i, lax.rem(r + rho, R), t), 0) + 1 - h, 0, 0, 0)

    def row_group(tab, i, k, t):
        return plan.shift_entry(tab, i, lax.rem(k + tab[plan.rho] + R, L), t)

    def turned(tab, x_ref, held, out):
        i = pl.program_id(0)
        _, _, kl = plan.place(tab)

        @pl.when(row_group(tab, i, pl.program_id(1), pl.program_id(2)) >= 0)
        def _():
            for r in range(R):
                for t in range(plan.cap_r):
                    a = plan.class_entry(tab, i, lax.rem(r + kl, R), t)

                    @pl.when(a >= 0)
                    def _(r=r, t=t, a=a):
                        out[r, 0, 0, 0, t, 0] = x_ref[0, 0, a].T

    def turned_map(i, k, t, tab):
        _, h, _ = plan.place(tab)
        return (i, 2 * jnp.maximum(row_group(tab, i, k, t), 0) + 1 - h, 0, 0, 0)

    partial = pl.pallas_call(
        direct,
        grid_spec=pltpu.PrefetchScalarGridSpec(
            num_scalar_prefetch=1,
            grid=(2, R, plan.cap_r),
            in_specs=[pl.BlockSpec(in_block, direct_map)],
            out_specs=pl.BlockSpec(
                (1, R, 1, 1, 1, plan.cap_l, TILE, TILE), lambda i, r, t, tab: (r, 0, i, 0, t, 0, 0, 0)
            ),
        ),
        out_shape=shape,
        compiler_params=pltpu.CompilerParams(vmem_limit_bytes=VMEM_LIMIT),
        name="pack_far_direct",
    )(table, updates)
    return pl.pallas_call(
        turned,
        grid_spec=pltpu.PrefetchScalarGridSpec(
            num_scalar_prefetch=1,
            grid=(2, R, plan.cap_l),
            in_specs=[pl.BlockSpec(in_block, turned_map), pl.BlockSpec(memory_space=pl.ANY)],
            out_specs=pl.BlockSpec(
                (R, 1, 1, 1, plan.cap_r, 1, TILE, TILE), lambda i, k, t, tab: (0, k, i, 1, 0, t, 0, 0)
            ),
        ),
        out_shape=shape,
        input_output_aliases={2: 0},
        compiler_params=pltpu.CompilerParams(vmem_limit_bytes=VMEM_LIMIT),
        name="pack_far_turned",
    )(table, updates, partial)


def pack_panel(plan, table, updates):
    R, L = plan.R, plan.L
    slots = updates.shape[2]

    def which(tab, i):
        rho, _, _ = plan.place(tab)
        a = tab[plan.first + i]
        s = plan.get_shift(tab, i, jnp.maximum(a, 0))
        low = modr(s - rho, L) < PT
        high = modr(s - rho - R, L) < PT
        return a, low, high

    def body(tab, x_ref, out):
        i = pl.program_id(0)
        a, low, high = which(tab, i)
        there = (a >= 0) & (low | high)

        for k in range(L):
            for t in range(plan.cap_l):
                b = plan.shift_entry(tab, i, lax.rem(tab[plan.kap] + k, L), t)

                @pl.when((b >= 0) & there)
                def _(k=k, t=t, b=b):
                    out[k, 0, t] = x_ref[0, 0, b]

    def in_map(i, tab):
        a, _, high = which(tab, i)
        return (i, 2 * jnp.maximum(a, 0) + high.astype(jnp.int32), 0, 0, 0)

    return pl.pallas_call(
        body,
        grid_spec=pltpu.PrefetchScalarGridSpec(
            num_scalar_prefetch=1,
            grid=(2,),
            in_specs=[pl.BlockSpec((1, 1, slots, TILE, TILE), in_map)],
            out_specs=pl.BlockSpec((L, 1, plan.cap_l, TILE, TILE), lambda i, tab: (0, i, 0, 0, 0)),
        ),
        out_shape=jax.ShapeDtypeStruct((L, 2, plan.cap_l, TILE, TILE), jnp.bfloat16),
        compiler_params=pltpu.CompilerParams(vmem_limit_bytes=VMEM_LIMIT),
        name="pack_panel",
    )(table, updates)


def assemble_panel(plan, table, front_rows, child_rows, slots):
    R, L = plan.R, plan.L

    def body(tab, f_ref, c0_ref, c1_ref, out):
        f = pl.program_id(0)
        for cs in range(slots):
            out[cs] = f_ref[0, pl.ds(cs, TILE, stride=slots), :]
        for i, c_ref in ((0, c0_ref), (1, c1_ref)):

            @pl.when(tab[plan.first + i] >= 0)
            def _(i=i, c_ref=c_ref):
                for k in range(L):
                    for t in range(plan.cap_l):
                        b = plan.shift_entry(tab, i, lax.rem(tab[plan.kap] + k, L), t)

                        @pl.when(b >= 0)
                        def _(k=k, t=t, b=b):
                            cs = plan.get_home(tab, i, b)
                            out[cs] = out[cs] + c_ref[0, k, 0, t].astype(jnp.float32)

    def child_map(i):
        def at(f, tab):
            s = plan.get_shift(tab, i, jnp.maximum(tab[plan.first + i], 0))
            return (lax.rem(modr(s - f, L), R), 0, i, 0, 0, 0)

        return at

    child_block = (1, L, 1, plan.cap_l, TILE, TILE)
    return pl.pallas_call(
        body,
        grid_spec=pltpu.PrefetchScalarGridSpec(
            num_scalar_prefetch=1,
            grid=(PT,),
            in_specs=[
                pl.BlockSpec((1, TILE * slots, TILE), lambda f, tab: (f, 0, 0)),
                pl.BlockSpec(child_block, child_map(0)),
                pl.BlockSpec(child_block, child_map(1)),
            ],
            out_specs=pl.BlockSpec((slots, TILE, TILE), lambda f, tab: (0, f, 0)),
        ),
        out_shape=jax.ShapeDtypeStruct((slots, PD, TILE), jnp.float32),
        compiler_params=pltpu.CompilerParams(vmem_limit_bytes=VMEM_LIMIT),
        name="assemble_panel",
    )(table, front_rows, child_rows, child_rows)


def split_bf16(x):
    high = x.astype(jnp.bfloat16)
    return high, (x - high.astype(jnp.float32)).astype(jnp.bfloat16)


def solve_blocks(inverse, blocks, wide):
    count = blocks.shape[0]
    pair = 2 if count % 2 == 0 else 1

    def body(inv, x, high, low, inv_high, inv_low):
        @pl.when(pl.program_id(0) == 0)
        def _():
            inv_high[...], inv_low[...] = split_bf16(inv[...])

        xs = [split_bf16(x[q]) for q in range(pair)]
        xh = jnp.concatenate([p[0] for p in xs], axis=1)
        xl = jnp.concatenate([p[1] for p in xs], axis=1)
        y = jnp.dot(inv_high[...], xh, preferred_element_type=jnp.float32)
        y += jnp.dot(inv_high[...], xl, preferred_element_type=jnp.float32)
        y += jnp.dot(inv_low[...], xh, preferred_element_type=jnp.float32)
        hi, lo = split_bf16(y)
        if wide:
            high[...], low[...] = hi, lo
        else:
            for q in range(pair):
                high[q], low[q] = hi[:, q * TILE : (q + 1) * TILE], lo[:, q * TILE : (q + 1) * TILE]

    if wide:
        shape, spec = (PD, count * TILE), pl.BlockSpec((PD, pair * TILE), lambda s: (0, s))
    else:
        shape, spec = (count, PD, TILE), pl.BlockSpec((pair, PD, TILE), lambda s: (s, 0, 0))
    whole = pl.BlockSpec((PD, PD), lambda s: (0, 0))
    return pl.pallas_call(
        body,
        grid=(count // pair,),
        in_specs=[whole, pl.BlockSpec((pair, PD, TILE), lambda s: (s, 0, 0))],
        out_specs=[spec, spec],
        out_shape=[jax.ShapeDtypeStruct(shape, jnp.bfloat16)] * 2,
        scratch_shapes=[pltpu.VMEM((PD, PD), jnp.bfloat16)] * 2,
        compiler_params=pltpu.CompilerParams(vmem_limit_bytes=VMEM_LIMIT),
        name="solve_blocks",
    )(inverse, blocks)


def slab_source(plan, tab, i, fr):
    a = tab[plan.at_home + i * plan.homes + fr // 2]
    lane = modr(plan.get_shift(tab, i, jnp.maximum(a, 0)) - tab[plan.rho] - plan.R * lax.rem(fr, 2), plan.L)
    return a, lax.rem(lane, plan.R), lane // plan.R


def add_blocks(plan, tab, i, fr, half, out, block, slots):
    R, L = plan.R, plan.L
    kap = tab[plan.kap]
    for k in range(R):
        for t in range(plan.cap_l):
            b = plan.shift_entry(tab, i, lax.rem(kap + half * R + k, L), t)
            cs = plan.get_home(tab, i, jnp.maximum(b, 0))

            @pl.when((b >= 0) & jnp.logical_not((cs == 0) & (kap < PT)))
            def _(k=k, t=t, cs=cs):
                at = pl.ds(cs, TILE, stride=slots)
                out[0, at, :] = out[0, at, :] + block(k, t).astype(jnp.float32)


def near_spec(plan, i):
    def at(fr, tab):
        a, low, half = slab_source(plan, tab, i, fr)
        rank = tab[plan.rank + i * plan.G + jnp.maximum(a, 0)]
        return (low, half, 0, i, rank, 0, 0, 0)

    return pl.BlockSpec((1, 1, plan.R, 1, 1, plan.cap_l, TILE, TILE), at)


def far_specs(plan, i):
    def direct(fr, tab):
        a, low, _ = slab_source(plan, tab, i, fr)
        return (low, 0, i, 0, tab[plan.rank + i * plan.G + jnp.maximum(a, 0)], 0, 0, 0)

    def turned(fr, tab):
        a, low, _ = slab_source(plan, tab, i, fr)
        return (0, low, i, 1, tab[plan.rank + i * plan.G + jnp.maximum(a, 0)], 0, 0, 0)

    return [
        pl.BlockSpec((1, plan.R, 1, 1, 1, plan.cap_l, TILE, TILE), direct),
        pl.BlockSpec((plan.R, 1, 1, 1, 1, plan.cap_l, TILE, TILE), turned),
    ]


def trailing(plan, table, front, factor, row_parts, col_parts, far, slots):
    R, L = plan.R, plan.L
    count = front.shape[0]
    per_lane = row_parts[0].shape[0] // 2

    def body(tab, f_ref, l_ref, rh, rl, ch, cl, direct0, turned0, direct1, turned1, out):
        fr = pl.program_id(0)
        rho, kap = tab[plan.rho], tab[plan.kap]
        head = (fr == 0) & (rho < PT)
        contract = (((0,), (0,)), ((), ()))
        step = 256 if slots % 2 == 0 else 128

        @pl.when(jnp.logical_not(head))
        def _():
            xh, xl = rh[0], rl[0]
            for w in range(slots * TILE // step):
                cols = pl.ds(w * step, step)
                y = lax.dot_general(xh, ch[:, cols], contract, preferred_element_type=jnp.float32)
                y += lax.dot_general(xh, cl[:, cols], contract, preferred_element_type=jnp.float32)
                y += lax.dot_general(xl, ch[:, cols], contract, preferred_element_type=jnp.float32)
                for q in range(step // TILE):
                    at = pl.ds(w * (step // TILE) + q, TILE, stride=slots)
                    out[0, at, :] = f_ref[0, at, :] - y[:, q * TILE : (q + 1) * TILE]

        h = kap // R
        for i, direct, turned in ((0, direct0, turned0), (1, direct1, turned1)):
            a, _, half = slab_source(plan, tab, i, fr)

            @pl.when((a >= 0) & jnp.logical_not(head) & (half != h))
            def _(i=i, direct=direct):
                add_blocks(plan, tab, i, fr, h, out, lambda k, t: direct[0, k, 0, 0, 0, t], slots)

            @pl.when((a >= 0) & jnp.logical_not(head) & (half == h))
            def _(i=i, turned=turned):
                add_blocks(plan, tab, i, fr, 1 - h, out, lambda k, t: turned[k, 0, 0, 0, 0, t], slots)

        @pl.when(head)
        def _():
            out[...] = jnp.zeros_like(out)

        @pl.when((kap < PT) & head)
        def _():
            out[0, pl.ds(0, TILE, stride=slots), :] = l_ref[...]

        @pl.when((kap < PT) & jnp.logical_not(head))
        def _():
            rows = pl.ds(pl.multiple_of(kap * TILE, TILE), TILE)
            x = rh[0, rows, :].astype(jnp.float32) + rl[0, rows, :].astype(jnp.float32)
            out[0, pl.ds(0, TILE, stride=slots), :] = x.T

    slab = pl.BlockSpec((1, TILE * slots, TILE), lambda fr, tab: (fr, 0, 0))
    row_spec = pl.BlockSpec((1, PD, TILE), lambda fr, tab: (lax.rem(fr, 2) * per_lane + fr // 2, 0, 0))
    col_spec = pl.BlockSpec((PD, slots * TILE), lambda fr, tab: (0, 0))
    factor_spec = pl.BlockSpec(
        (TILE, TILE), lambda fr, tab: (jnp.minimum(tab[plan.rho], PT - 1), jnp.minimum(tab[plan.kap], PT - 1))
    )
    flops = 6 * count * TILE * PD * slots * TILE
    return pl.pallas_call(
        body,
        grid_spec=pltpu.PrefetchScalarGridSpec(
            num_scalar_prefetch=1,
            grid=(count,),
            in_specs=[slab, factor_spec, row_spec, row_spec, col_spec, col_spec] + far_specs(plan, 0) + far_specs(plan, 1),
            out_specs=slab,
        ),
        out_shape=jax.ShapeDtypeStruct(front.shape, jnp.float32),
        compiler_params=pltpu.CompilerParams(vmem_limit_bytes=VMEM_LIMIT),
        cost_estimate=pl.CostEstimate(flops=flops, bytes_accessed=2 * front.size * 4, transcendentals=0),
        name="trailing",
    )(table, front, factor, *row_parts, *col_parts, far, far, far, far)


def add_near(plan, table, total, near, slots):
    def body(tab, t_ref, near0, near1, out):
        fr = pl.program_id(0)
        out[...] = t_ref[...]
        live = jnp.logical_not((fr == 0) & (tab[plan.rho] < PT))
        for i, near_ref in ((0, near0), (1, near1)):
            a, _, half = slab_source(plan, tab, i, fr)

            @pl.when(live & (a >= 0))
            def _(i=i, half=half, near_ref=near_ref):
                add_blocks(plan, tab, i, fr, half, out, lambda k, t: near_ref[0, 0, k, 0, 0, t], slots)

    slab = pl.BlockSpec((1, TILE * slots, TILE), lambda fr, tab: (fr, 0, 0))
    return pl.pallas_call(
        body,
        grid_spec=pltpu.PrefetchScalarGridSpec(
            num_scalar_prefetch=1,
            grid=(total.shape[0],),
            in_specs=[slab, near_spec(plan, 0), near_spec(plan, 1)],
            out_specs=slab,
        ),
        out_shape=jax.ShapeDtypeStruct(total.shape, jnp.float32),
        input_output_aliases={1: 0},
        compiler_params=pltpu.CompilerParams(vmem_limit_bytes=VMEM_LIMIT),
        name="add_near",
    )(table, total, near, near)


def permute(x, plan, target):
    R, L = plan.R, plan.L
    pairs = []
    for rho in range(R):
        for h in range(2):
            for kl in range(R):
                r2, h2, k2 = target(rho, h, kl)
                pairs.append((rho * L + h * R + kl, (r2 % R) * L + h2 * R + k2 % R))
    return lax.ppermute(x, AXES, pairs)


def panel_factor(diagonal):
    factor = jnp.linalg.cholesky(diagonal)
    inverse = lax.linalg.triangular_solve(
        factor, jnp.eye(PD, dtype=jnp.float32), left_side=True, lower=True
    )
    return factor, inverse


def scaled_half(block, largest):
    exponent = jnp.clip(jnp.ceil(jnp.log2(jnp.maximum(largest, 1e-30))), -100.0, 100.0)
    scaled = (block * jnp.exp2(-exponent)).astype(jnp.float16)
    return jnp.concatenate([scaled, jnp.full((16, TILE), exponent, jnp.float16)], axis=0)


def from_half(parts):
    exponent = parts[:, -1:, :1].astype(jnp.float32)
    return parts[:, :-16].astype(jnp.float32) * jnp.exp2(exponent)


def on_device(front_blocks, child_updates, child_map):
    R, L = lax.axis_size("row"), lax.axis_size(COL)
    front_rows, tile, slots, _ = front_blocks.shape
    plan = Plan(R, L, child_map.shape[1] // L, slots)
    table = make_table(plan, child_map)
    front = front_blocks.reshape(front_rows, tile * slots, tile)
    updates = jnp.transpose(child_updates, (0, 1, 3, 2, 4))

    table, first = lax.optimization_barrier((table, front[0]))
    front_head = lax.all_gather(first, "row")
    head = pack_panel(plan, table, updates)
    moved = lax.all_to_all(head, COL, 0, 0, tiled=True)

    def exchange(blocks, axes, count, after):
        flat, _ = lax.optimization_barrier((blocks.reshape((count, -1, TILE, TILE)), after))
        return lax.all_to_all(flat, axes, 0, 0, tiled=True).reshape(blocks.shape)

    far = pack_far(plan, table, updates)
    far_in = exchange(far, ("row", "lane"), R * R, (moved, front_head))

    child_head = lax.all_gather(moved, "row")
    near = pack_near(plan, table, updates)
    child_head, near = lax.optimization_barrier((child_head, near))
    panel = assemble_panel(plan, table, front_head, child_head, slots)
    diag_tiles = lax.all_gather(panel[0], COL)
    diagonal = jnp.concatenate([diag_tiles[k] for k in range(PT)], axis=1)
    count = slots // R
    piece = lax.dynamic_slice_in_dim(panel, lax.axis_index("row") * count, count, axis=0)
    piece = scaled_half(piece.reshape(count * PD, TILE), jnp.max(jnp.abs(panel)))
    piece, far_in = lax.optimization_barrier((piece, far_in))
    piece = permute(piece, plan, lambda rho, h, kl: (kl, h, rho))
    row_half = lax.all_gather(piece, COL)
    near_in = exchange(near, AXES, R * L, (row_half, diagonal))
    row_panel = from_half(row_half).reshape(L * count, PD, TILE)

    factor, inverse = panel_factor(diagonal)
    col_parts = solve_blocks(inverse, panel, True)
    row_parts = solve_blocks(inverse, row_panel, False)
    total = trailing(plan, table, front, factor, row_parts, col_parts, far_in, slots)
    near_in, total = lax.optimization_barrier((near_in, total))
    total = add_near(plan, table, total, near_in, slots)
    return total.reshape(front_blocks.shape)


def solution(mesh):
    rows, lanes = mesh.devices.shape
    split = Mesh(mesh.devices.reshape(rows, 2, lanes // 2), AXES)
    placed = (P(None, "row", None, COL), P(None, None, "row", None, COL), P())
    return jax.shard_map(
        on_device,
        mesh=split,
        in_specs=placed,
        out_specs=P(None, "row", None, COL),
        check_vma=False,
    )
```

```python
import functools

import jax
import jax.numpy as jnp
from jax import lax
from jax.experimental import pallas as pl
from jax.experimental.pallas import tpu as pltpu
from jax.sharding import Mesh, PartitionSpec as P

PD = 512
TILE = 128
PT = PD // TILE
COL = ("half", "lane")
AXES = ("row",) + COL
VMEM_LIMIT = 48 * 1024 * 1024
STREAMS = 4


class Plan:
    def __init__(self, rows, lanes, groups, homes):
        self.R, self.L, self.G = rows, lanes, groups
        self.cap_r = -(-groups // rows)
        self.cap_l = -(-groups // lanes)
        self.shift = 0
        self.home = self.shift + 2 * groups
        self.by_class = self.home + 2 * groups
        self.by_shift = self.by_class + 2 * rows * self.cap_r
        self.first = self.by_shift + 2 * lanes * self.cap_l
        self.homes = homes
        self.at_home = self.first + 2
        self.rank = self.at_home + 2 * homes
        self.rho = self.rank + 2 * groups
        self.kap = self.rho + 1

    def get_shift(self, tab, i, a):
        return tab[self.shift + i * self.G + a]

    def get_home(self, tab, i, a):
        return tab[self.home + i * self.G + a]

    def class_entry(self, tab, i, m, t):
        return tab[self.by_class + (i * self.R + m) * self.cap_r + t]

    def shift_entry(self, tab, i, s, t):
        return tab[self.by_shift + (i * self.L + s) * self.cap_l + t]

    def place(self, tab):
        kap = tab[self.kap]
        return tab[self.rho], kap // self.R, lax.rem(kap, self.R)


def make_table(plan, child_map):
    R, L, G = plan.R, plan.L, plan.G
    lead = child_map.reshape(2, G, L)[:, :, 0]
    shift, home = lead % L, lead // L
    ids = jnp.arange(G, dtype=jnp.int32)
    before = ids[None, :] < ids[:, None]

    def inverse(keys, count, capacity):
        rank = jnp.sum((keys[:, :, None] == keys[:, None, :]) & before[None], axis=2)
        hit = (keys[:, None, None, :] == jnp.arange(count)[None, :, None, None]) & (
            rank[:, None, None, :] == jnp.arange(capacity)[None, None, :, None]
        )
        return jnp.max(jnp.where(hit, ids[None, None, None, :], -1), axis=3)

    at_home = inverse(home, plan.homes, 1)
    same = (shift % R)[:, :, None] == (shift % R)[:, None, :]
    rank = jnp.sum(same & before[None], axis=2)
    parts = [shift, home, inverse(shift % R, R, plan.cap_r), inverse(shift, L, plan.cap_l), at_home[:, 0], at_home, rank]
    here = [lax.axis_index("row"), lax.axis_index(COL)]
    return jnp.concatenate(
        [p.reshape(-1).astype(jnp.int32) for p in parts] + [h.reshape(1).astype(jnp.int32) for h in here]
    )


def modr(value, n):
    return lax.rem(value + 2 * n, n)


def pack_near(plan, table, updates):
    R, L = plan.R, plan.L
    slots = updates.shape[2]

    def body(tab, x_ref, out):
        i = pl.program_id(0)
        kap = tab[plan.kap]
        for k in range(L):
            for t in range(plan.cap_l):
                b = plan.shift_entry(tab, i, lax.rem(kap + k, L), t)

                @pl.when(b >= 0)
                def _(k=k, t=t, b=b):
                    out[0, k // R, k % R, 0, 0, t] = x_ref[0, 0, b]

    def in_map(i, r, t, tab):
        rho, h, _ = plan.place(tab)
        return (i, 2 * jnp.maximum(plan.class_entry(tab, i, lax.rem(r + rho, R), t), 0) + h, 0, 0, 0)

    shape = (R, 2, R, 2, plan.cap_r, plan.cap_l, TILE, TILE)
    return pl.pallas_call(
        body,
        grid_spec=pltpu.PrefetchScalarGridSpec(
            num_scalar_prefetch=1,
            grid=(2, R, plan.cap_r),
            in_specs=[pl.BlockSpec((1, 1, slots, TILE, TILE), in_map)],
            out_specs=pl.BlockSpec(
                (1, 2, R, 1, 1, plan.cap_l, TILE, TILE), lambda i, r, t, tab: (r, 0, 0, i, t, 0, 0, 0)
            ),
        ),
        out_shape=jax.ShapeDtypeStruct(shape, jnp.bfloat16),
        compiler_params=pltpu.CompilerParams(vmem_limit_bytes=VMEM_LIMIT),
        name="pack_near",
    )(table, updates)


def pack_far(plan, table, updates):
    R, L = plan.R, plan.L
    slots = updates.shape[2]
    shape = jax.ShapeDtypeStruct((R, R, 2, 2, plan.cap_r, plan.cap_l, TILE, TILE), jnp.bfloat16)
    in_block = (1, 1, slots, TILE, TILE)

    def direct(tab, x_ref, out):
        i = pl.program_id(0)
        kap = tab[plan.kap]
        h = kap // R
        for k in range(R):
            for t in range(plan.cap_l):
                b = plan.shift_entry(tab, i, lax.rem(kap + h * R + k, L), t)

                @pl.when(b >= 0)
                def _(k=k, t=t, b=b):
                    out[0, k, 0, 0, 0, t] = x_ref[0, 0, b]

    def direct_map(i, r, t, tab):
        rho, h, _ = plan.place(tab)
        return (i, 2 * jnp.maximum(plan.class_entry(tab, i, lax.rem(r + rho, R), t), 0) + 1 - h, 0, 0, 0)

    def row_group(tab, i, k, t):
        return plan.shift_entry(tab, i, lax.rem(k + tab[plan.rho] + R, L), t)

    def turned(tab, x_ref, held, out):
        i = pl.program_id(0)
        _, _, kl = plan.place(tab)

        @pl.when(row_group(tab, i, pl.program_id(1), pl.program_id(2)) >= 0)
        def _():
            for r in range(R):
                for t in range(plan.cap_r):
                    a = plan.class_entry(tab, i, lax.rem(r + kl, R), t)

                    @pl.when(a >= 0)
                    def _(r=r, t=t, a=a):
                        out[r, 0, 0, 0, t, 0] = x_ref[0, 0, a].T

    def turned_map(i, k, t, tab):
        _, h, _ = plan.place(tab)
        return (i, 2 * jnp.maximum(row_group(tab, i, k, t), 0) + 1 - h, 0, 0, 0)

    partial = pl.pallas_call(
        direct,
        grid_spec=pltpu.PrefetchScalarGridSpec(
            num_scalar_prefetch=1,
            grid=(2, R, plan.cap_r),
            in_specs=[pl.BlockSpec(in_block, direct_map)],
            out_specs=pl.BlockSpec(
                (1, R, 1, 1, 1, plan.cap_l, TILE, TILE), lambda i, r, t, tab: (r, 0, i, 0, t, 0, 0, 0)
            ),
        ),
        out_shape=shape,
        compiler_params=pltpu.CompilerParams(vmem_limit_bytes=VMEM_LIMIT),
        name="pack_far_direct",
    )(table, updates)
    return pl.pallas_call(
        turned,
        grid_spec=pltpu.PrefetchScalarGridSpec(
            num_scalar_prefetch=1,
            grid=(2, R, plan.cap_l),
            in_specs=[pl.BlockSpec(in_block, turned_map), pl.BlockSpec(memory_space=pl.ANY)],
            out_specs=pl.BlockSpec(
                (R, 1, 1, 1, plan.cap_r, 1, TILE, TILE), lambda i, k, t, tab: (0, k, i, 1, 0, t, 0, 0)
            ),
        ),
        out_shape=shape,
        input_output_aliases={2: 0},
        compiler_params=pltpu.CompilerParams(vmem_limit_bytes=VMEM_LIMIT),
        name="pack_far_turned",
    )(table, updates, partial)


def pack_panel(plan, table, updates):
    R, L = plan.R, plan.L
    slots = updates.shape[2]

    def which(tab, i):
        rho, _, _ = plan.place(tab)
        a = tab[plan.first + i]
        s = plan.get_shift(tab, i, jnp.maximum(a, 0))
        low = modr(s - rho, L) < PT
        high = modr(s - rho - R, L) < PT
        return a, low, high

    def body(tab, x_ref, out):
        i = pl.program_id(0)
        a, low, high = which(tab, i)
        there = (a >= 0) & (low | high)

        for k in range(L):
            for t in range(plan.cap_l):
                b = plan.shift_entry(tab, i, lax.rem(tab[plan.kap] + k, L), t)

                @pl.when((b >= 0) & there)
                def _(k=k, t=t, b=b):
                    out[k, 0, t] = x_ref[0, 0, b]

    def in_map(i, tab):
        a, _, high = which(tab, i)
        return (i, 2 * jnp.maximum(a, 0) + high.astype(jnp.int32), 0, 0, 0)

    return pl.pallas_call(
        body,
        grid_spec=pltpu.PrefetchScalarGridSpec(
            num_scalar_prefetch=1,
            grid=(2,),
            in_specs=[pl.BlockSpec((1, 1, slots, TILE, TILE), in_map)],
            out_specs=pl.BlockSpec((L, 1, plan.cap_l, TILE, TILE), lambda i, tab: (0, i, 0, 0, 0)),
        ),
        out_shape=jax.ShapeDtypeStruct((L, 2, plan.cap_l, TILE, TILE), jnp.bfloat16),
        compiler_params=pltpu.CompilerParams(vmem_limit_bytes=VMEM_LIMIT),
        name="pack_panel",
    )(table, updates)


def assemble_panel(plan, table, front_rows, child_rows, slots):
    R, L = plan.R, plan.L

    def body(tab, f_ref, c0_ref, c1_ref, out):
        f = pl.program_id(0)
        for cs in range(slots):
            out[cs] = f_ref[0, pl.ds(cs, TILE, stride=slots), :]
        for i, c_ref in ((0, c0_ref), (1, c1_ref)):

            @pl.when(tab[plan.first + i] >= 0)
            def _(i=i, c_ref=c_ref):
                for k in range(L):
                    for t in range(plan.cap_l):
                        b = plan.shift_entry(tab, i, lax.rem(tab[plan.kap] + k, L), t)

                        @pl.when(b >= 0)
                        def _(k=k, t=t, b=b):
                            cs = plan.get_home(tab, i, b)
                            out[cs] = out[cs] + c_ref[0, k, 0, t].astype(jnp.float32)

    def child_map(i):
        def at(f, tab):
            s = plan.get_shift(tab, i, jnp.maximum(tab[plan.first + i], 0))
            return (lax.rem(modr(s - f, L), R), 0, i, 0, 0, 0)

        return at

    child_block = (1, L, 1, plan.cap_l, TILE, TILE)
    return pl.pallas_call(
        body,
        grid_spec=pltpu.PrefetchScalarGridSpec(
            num_scalar_prefetch=1,
            grid=(PT,),
            in_specs=[
                pl.BlockSpec((1, TILE * slots, TILE), lambda f, tab: (f, 0, 0)),
                pl.BlockSpec(child_block, child_map(0)),
                pl.BlockSpec(child_block, child_map(1)),
            ],
            out_specs=pl.BlockSpec((slots, TILE, TILE), lambda f, tab: (0, f, 0)),
        ),
        out_shape=jax.ShapeDtypeStruct((slots, PD, TILE), jnp.float32),
        compiler_params=pltpu.CompilerParams(vmem_limit_bytes=VMEM_LIMIT),
        name="assemble_panel",
    )(table, front_rows, child_rows, child_rows)


def split_bf16(x):
    high = x.astype(jnp.bfloat16)
    return high, (x - high.astype(jnp.float32)).astype(jnp.bfloat16)


def solve_blocks(inverse, blocks, wide):
    count = blocks.shape[0]
    pair = 2 if count % 2 == 0 else 1
    height = blocks.shape[1]

    def body(inv, x, high, low, inv_high, inv_low):
        @pl.when(pl.program_id(0) == 0)
        def _():
            inv_high[...], inv_low[...] = split_bf16(inv[...])

        xs = [split_bf16(x[q] if height == PD else decode(x[q])) for q in range(pair)]
        xh = jnp.concatenate([p[0] for p in xs], axis=1)
        xl = jnp.concatenate([p[1] for p in xs], axis=1)
        y = jnp.dot(inv_high[...], xh, preferred_element_type=jnp.float32)
        y += jnp.dot(inv_high[...], xl, preferred_element_type=jnp.float32)
        y += jnp.dot(inv_low[...], xh, preferred_element_type=jnp.float32)
        hi, lo = split_bf16(y)
        if wide:
            high[...], low[...] = hi, lo
        else:
            for q in range(pair):
                high[q], low[q] = hi[:, q * TILE : (q + 1) * TILE], lo[:, q * TILE : (q + 1) * TILE]

    if wide:
        shape, spec = (PD, count * TILE), pl.BlockSpec((PD, pair * TILE), lambda s: (0, s))
    else:
        shape, spec = (count, PD, TILE), pl.BlockSpec((pair, PD, TILE), lambda s: (s, 0, 0))
    whole = pl.BlockSpec((PD, PD), lambda s: (0, 0))
    return pl.pallas_call(
        body,
        grid=(count // pair,),
        in_specs=[whole, pl.BlockSpec((pair, height, TILE), lambda s: (s, 0, 0))],
        out_specs=[spec, spec],
        out_shape=[jax.ShapeDtypeStruct(shape, jnp.bfloat16)] * 2,
        scratch_shapes=[pltpu.VMEM((PD, PD), jnp.bfloat16)] * 2,
        compiler_params=pltpu.CompilerParams(vmem_limit_bytes=VMEM_LIMIT),
        name="solve_blocks",
    )(inverse, blocks)


def slab_source(plan, tab, i, fr):
    a = tab[plan.at_home + i * plan.homes + fr // 2]
    lane = modr(plan.get_shift(tab, i, jnp.maximum(a, 0)) - tab[plan.rho] - plan.R * lax.rem(fr, 2), plan.L)
    return a, lax.rem(lane, plan.R), lane // plan.R


def add_blocks(plan, tab, i, fr, half, out, block, slots):
    R, L = plan.R, plan.L
    kap = tab[plan.kap]
    for k in range(R):
        for t in range(plan.cap_l):
            b = plan.shift_entry(tab, i, lax.rem(kap + half * R + k, L), t)
            cs = plan.get_home(tab, i, jnp.maximum(b, 0))

            @pl.when((b >= 0) & jnp.logical_not((cs == 0) & (kap < PT)))
            def _(k=k, t=t, cs=cs):
                at = pl.ds(cs, TILE, stride=slots)
                out[at, :] = out[at, :] + block(k, t).astype(jnp.float32)


def far_specs(plan, i):
    def direct(fr, tab):
        a, low, _ = slab_source(plan, tab, i, fr)
        return (low, 0, i, 0, tab[plan.rank + i * plan.G + jnp.maximum(a, 0)], 0, 0, 0)

    def turned(fr, tab):
        a, low, _ = slab_source(plan, tab, i, fr)
        return (0, low, i, 1, tab[plan.rank + i * plan.G + jnp.maximum(a, 0)], 0, 0, 0)

    return [
        pl.BlockSpec((1, plan.R, 1, 1, 1, plan.cap_l, TILE, TILE), direct),
        pl.BlockSpec((plan.R, 1, 1, 1, 1, plan.cap_l, TILE, TILE), turned),
    ]


def trailing(plan, table, front, factor, row_parts, col_parts, far, slots):
    R, L = plan.R, plan.L
    count = front.shape[0]
    per_lane = row_parts[0].shape[0] // 2

    def body(tab, f_ref, l_ref, rh, rl, ch, cl, direct0, turned0, direct1, turned1, out):
        fr = pl.program_id(0)
        rho, kap = tab[plan.rho], tab[plan.kap]
        head = (fr == 0) & (rho < PT)
        contract = (((0,), (0,)), ((), ()))
        step = 256 if slots % 2 == 0 else 128

        @pl.when(jnp.logical_not(head))
        def _():
            xh, xl = rh[0], rl[0]
            for w in range(slots * TILE // step):
                cols = pl.ds(w * step, step)
                y = lax.dot_general(xh, ch[:, cols], contract, preferred_element_type=jnp.float32)
                y += lax.dot_general(xh, cl[:, cols], contract, preferred_element_type=jnp.float32)
                y += lax.dot_general(xl, ch[:, cols], contract, preferred_element_type=jnp.float32)
                for q in range(step // TILE):
                    at = pl.ds(w * (step // TILE) + q, TILE, stride=slots)
                    out[0, at, :] = f_ref[0, at, :] - y[:, q * TILE : (q + 1) * TILE]

        h = kap // R
        for i, direct, turned in ((0, direct0, turned0), (1, direct1, turned1)):
            a, _, half = slab_source(plan, tab, i, fr)

            @pl.when((a >= 0) & jnp.logical_not(head) & (half != h))
            def _(i=i, direct=direct):
                add_blocks(plan, tab, i, fr, h, out.at[0], lambda k, t: direct[0, k, 0, 0, 0, t], slots)

            @pl.when((a >= 0) & jnp.logical_not(head) & (half == h))
            def _(i=i, turned=turned):
                add_blocks(plan, tab, i, fr, 1 - h, out.at[0], lambda k, t: turned[k, 0, 0, 0, 0, t], slots)

        @pl.when(head)
        def _():
            out[...] = jnp.zeros_like(out)

        @pl.when((kap < PT) & head)
        def _():
            out[0, pl.ds(0, TILE, stride=slots), :] = l_ref[...]

        @pl.when((kap < PT) & jnp.logical_not(head))
        def _():
            rows = pl.ds(pl.multiple_of(kap * TILE, TILE), TILE)
            x = rh[0, rows, :].astype(jnp.float32) + rl[0, rows, :].astype(jnp.float32)
            out[0, pl.ds(0, TILE, stride=slots), :] = x.T

    slab = pl.BlockSpec((1, TILE * slots, TILE), lambda fr, tab: (fr, 0, 0))
    row_spec = pl.BlockSpec((1, PD, TILE), lambda fr, tab: (lax.rem(fr, 2) * per_lane + fr // 2, 0, 0))
    col_spec = pl.BlockSpec((PD, slots * TILE), lambda fr, tab: (0, 0))
    factor_spec = pl.BlockSpec(
        (TILE, TILE), lambda fr, tab: (jnp.minimum(tab[plan.rho], PT - 1), jnp.minimum(tab[plan.kap], PT - 1))
    )
    flops = 6 * count * TILE * PD * slots * TILE
    return pl.pallas_call(
        body,
        grid_spec=pltpu.PrefetchScalarGridSpec(
            num_scalar_prefetch=1,
            grid=(count,),
            in_specs=[slab, factor_spec, row_spec, row_spec, col_spec, col_spec] + far_specs(plan, 0) + far_specs(plan, 1),
            out_specs=slab,
        ),
        out_shape=jax.ShapeDtypeStruct(front.shape, jnp.float32),
        compiler_params=pltpu.CompilerParams(vmem_limit_bytes=VMEM_LIMIT),
        cost_estimate=pl.CostEstimate(flops=flops, bytes_accessed=2 * front.size * 4, transcendentals=0),
        name="trailing",
    )(table, front, factor, *row_parts, *col_parts, far, far, far, far)


def add_near(plan, table, total, near, slots):
    R = plan.R
    count, rows = total.shape[0], TILE * slots
    part = rows // STREAMS

    def body(tab, t_hbm, near_hbm, out_hbm, slab, blocks, load_sem, near_sem, store_sem):
        def loads(s, slot):
            copies = []
            for c in range(STREAMS):
                at = pl.ds(c * part, part)
                copies.append(
                    pltpu.make_async_copy(t_hbm.at[s, at], slab.at[slot, at], load_sem.at[slot, c])
                )
            for i in range(2):
                a, low, half = slab_source(plan, tab, i, s)
                rank = tab[plan.rank + i * plan.G + jnp.maximum(a, 0)]
                copies.append(
                    pltpu.make_async_copy(
                        near_hbm.at[low, half, :, i, rank], blocks.at[slot, i], near_sem.at[slot, i]
                    )
                )
            return copies

        def stores(s, slot):
            copies = []
            for c in range(STREAMS):
                at = pl.ds(c * part, part)
                copies.append(
                    pltpu.make_async_copy(slab.at[slot, at], out_hbm.at[s, at], store_sem.at[slot, c])
                )
            return copies

        def start(copies):
            for copy in copies:
                copy.start()

        def wait(copies):
            for copy in copies:
                copy.wait()

        start(loads(0, 0))
        start(loads(1, 1))

        def step(s, carry):
            slot = lax.rem(s, 4)
            ahead = lax.rem(s + 2, 4)

            @pl.when(s + 2 < count)
            def _():
                @pl.when(s >= 2)
                def _():
                    wait(stores(s - 2, ahead))

                start(loads(s + 2, ahead))

            wait(loads(s, slot))
            live = jnp.logical_not((s == 0) & (tab[plan.rho] < PT))
            for i in range(2):
                a, _, half = slab_source(plan, tab, i, s)

                @pl.when(live & (a >= 0))
                def _(i=i, half=half):
                    add_blocks(
                        plan, tab, i, s, half, slab.at[slot], lambda k, t: blocks[slot, i, k, t], slots
                    )

            start(stores(s, slot))
            return carry

        lax.fori_loop(0, count, step, 0)
        for s in range(count - 4, count):
            wait(stores(s, s % 4))

    hbm = pl.BlockSpec(memory_space=pl.ANY)
    return pl.pallas_call(
        body,
        grid_spec=pltpu.PrefetchScalarGridSpec(
            num_scalar_prefetch=1,
            grid=(1,),
            in_specs=[hbm, hbm],
            out_specs=hbm,
            scratch_shapes=[
                pltpu.VMEM((4, rows, TILE), jnp.float32),
                pltpu.VMEM((4, 2, R, plan.cap_l, TILE, TILE), jnp.bfloat16),
                pltpu.SemaphoreType.DMA((4, STREAMS)),
                pltpu.SemaphoreType.DMA((4, 2)),
                pltpu.SemaphoreType.DMA((4, STREAMS)),
            ],
        ),
        out_shape=jax.ShapeDtypeStruct(total.shape, jnp.float32),
        input_output_aliases={1: 0},
        compiler_params=pltpu.CompilerParams(vmem_limit_bytes=VMEM_LIMIT),
        name="add_near",
    )(table, total, near)


def permute(x, plan, target):
    R, L = plan.R, plan.L
    pairs = []
    for rho in range(R):
        for h in range(2):
            for kl in range(R):
                r2, h2, k2 = target(rho, h, kl)
                pairs.append((rho * L + h * R + kl, (r2 % R) * L + h2 * R + k2 % R))
    return lax.ppermute(x, AXES, pairs)


def panel_factor(diagonal):
    factor = jnp.linalg.cholesky(diagonal)
    inverse = lax.linalg.triangular_solve(
        factor, jnp.eye(PD, dtype=jnp.float32), left_side=True, lower=True
    )
    return factor, inverse


def encode(blocks):
    largest = jnp.max(jnp.abs(blocks), axis=1, keepdims=True)
    exponent = jnp.clip(jnp.ceil(jnp.log2(jnp.maximum(largest, 1e-30))), -100.0, 100.0)
    fixed = jnp.clip(jnp.round(blocks * jnp.exp2(15.0 - exponent)), -32767.0, 32767.0).astype(jnp.int32)
    words = (fixed[:, : PD // 2] << 16) | (fixed[:, PD // 2 :] & 0xFFFF)
    tail = jnp.broadcast_to(exponent.astype(jnp.int32), (blocks.shape[0], 8, TILE))
    return jnp.concatenate([words, tail], axis=1)


def decode(words):
    scale = jnp.exp2((words[PD // 2 : PD // 2 + 1] - 15).astype(jnp.float32))
    pairs = words[: PD // 2]
    fixed = jnp.concatenate([pairs >> 16, (pairs << 16) >> 16], axis=0)
    return fixed.astype(jnp.float32) * scale


def on_device(front_blocks, child_updates, child_map):
    R, L = lax.axis_size("row"), lax.axis_size(COL)
    front_rows, tile, slots, _ = front_blocks.shape
    plan = Plan(R, L, child_map.shape[1] // L, slots)
    table = make_table(plan, child_map)
    front = front_blocks.reshape(front_rows, tile * slots, tile)
    updates = jnp.transpose(child_updates, (0, 1, 3, 2, 4))

    head = pack_panel(plan, table, updates)
    table, first = lax.optimization_barrier((table, front[0]))
    front_head = lax.all_gather(first, "row")
    moved = lax.all_to_all(head, COL, 0, 0, tiled=True)

    def exchange(blocks, axes, count, after):
        flat, _ = lax.optimization_barrier((blocks.reshape((count, -1, TILE, TILE)), after))
        return lax.all_to_all(flat, axes, 0, 0, tiled=True).reshape(blocks.shape)

    far = pack_far(plan, table, updates)
    far_in = exchange(far, ("row", "lane"), R * R, (moved, front_head))

    child_head = lax.all_gather(moved, "row")
    near = pack_near(plan, table, updates)
    child_head, near = lax.optimization_barrier((child_head, near))
    panel = assemble_panel(plan, table, front_head, child_head, slots)
    diag_tiles = lax.all_gather(panel[0], COL)
    count = slots // R
    piece = encode(lax.dynamic_slice_in_dim(panel, lax.axis_index("row") * count, count, axis=0))
    piece = permute(piece, plan, lambda rho, h, kl: (kl, h, rho))
    diagonal = jnp.concatenate([diag_tiles[k] for k in range(PT)], axis=1)
    diagonal, piece = lax.optimization_barrier((diagonal, piece))
    near_in = exchange(near, AXES, R * L, piece)
    row_panel = lax.all_gather(piece, COL, tiled=True)

    factor, inverse = panel_factor(diagonal)
    col_parts = solve_blocks(inverse, panel, True)
    row_parts = solve_blocks(inverse, row_panel, False)
    total = trailing(plan, table, front, factor, row_parts, col_parts, far_in, slots)
    near_in, total = lax.optimization_barrier((near_in, total))
    total = add_near(plan, table, total, near_in, slots)
    return total.reshape(front_blocks.shape)


def solution(mesh):
    rows, lanes = mesh.devices.shape
    split = Mesh(mesh.devices.reshape(rows, 2, lanes // 2), AXES)
    placed = (P(None, "row", None, COL), P(None, None, "row", None, COL), P())
    return jax.shard_map(
        on_device,
        mesh=split,
        in_specs=placed,
        out_specs=P(None, "row", None, COL),
        check_vma=False,
    )
```

```python
import functools

import jax
import jax.numpy as jnp
from jax import lax
from jax.experimental import pallas as pl
from jax.experimental.pallas import tpu as pltpu
from jax.sharding import Mesh, PartitionSpec as P

PD = 512
TILE = 128
PT = PD // TILE
COL = ("half", "lane")
AXES = ("row",) + COL
VMEM_LIMIT = 48 * 1024 * 1024
STREAMS = 4


class Plan:
    def __init__(self, rows, lanes, groups, homes):
        self.R, self.L, self.G = rows, lanes, groups
        self.cap_r = -(-groups // rows)
        self.cap_l = -(-groups // lanes)
        self.shift = 0
        self.home = self.shift + 2 * groups
        self.by_class = self.home + 2 * groups
        self.by_shift = self.by_class + 2 * rows * self.cap_r
        self.first = self.by_shift + 2 * lanes * self.cap_l
        self.homes = homes
        self.at_home = self.first + 2
        self.rank = self.at_home + 2 * homes
        self.rho = self.rank + 2 * groups
        self.kap = self.rho + 1

    def get_shift(self, tab, i, a):
        return tab[self.shift + i * self.G + a]

    def get_home(self, tab, i, a):
        return tab[self.home + i * self.G + a]

    def class_entry(self, tab, i, m, t):
        return tab[self.by_class + (i * self.R + m) * self.cap_r + t]

    def shift_entry(self, tab, i, s, t):
        return tab[self.by_shift + (i * self.L + s) * self.cap_l + t]

    def place(self, tab):
        kap = tab[self.kap]
        return tab[self.rho], kap // self.R, lax.rem(kap, self.R)


def make_table(plan, child_map):
    R, L, G = plan.R, plan.L, plan.G
    lead = child_map.reshape(2, G, L)[:, :, 0]
    shift, home = lead % L, lead // L
    ids = jnp.arange(G, dtype=jnp.int32)
    before = ids[None, :] < ids[:, None]

    def inverse(keys, count, capacity):
        rank = jnp.sum((keys[:, :, None] == keys[:, None, :]) & before[None], axis=2)
        hit = (keys[:, None, None, :] == jnp.arange(count)[None, :, None, None]) & (
            rank[:, None, None, :] == jnp.arange(capacity)[None, None, :, None]
        )
        return jnp.max(jnp.where(hit, ids[None, None, None, :], -1), axis=3)

    at_home = inverse(home, plan.homes, 1)
    same = (shift % R)[:, :, None] == (shift % R)[:, None, :]
    rank = jnp.sum(same & before[None], axis=2)
    parts = [shift, home, inverse(shift % R, R, plan.cap_r), inverse(shift, L, plan.cap_l), at_home[:, 0], at_home, rank]
    here = [lax.axis_index("row"), lax.axis_index(COL)]
    return jnp.concatenate(
        [p.reshape(-1).astype(jnp.int32) for p in parts] + [h.reshape(1).astype(jnp.int32) for h in here]
    )


def modr(value, n):
    return lax.rem(value + 2 * n, n)


def pack_near(plan, table, updates):
    R, L = plan.R, plan.L
    slots = updates.shape[2]

    def body(tab, x_ref, out):
        i = pl.program_id(0)
        kap = tab[plan.kap]
        for k in range(L):
            for t in range(plan.cap_l):
                b = plan.shift_entry(tab, i, lax.rem(kap + k, L), t)

                @pl.when(b >= 0)
                def _(k=k, t=t, b=b):
                    out[0, k // R, k % R, 0, 0, t] = x_ref[0, 0, b]

    def in_map(i, r, t, tab):
        rho, h, _ = plan.place(tab)
        return (i, 2 * jnp.maximum(plan.class_entry(tab, i, lax.rem(r + rho, R), t), 0) + h, 0, 0, 0)

    shape = (R, 2, R, 2, plan.cap_r, plan.cap_l, TILE, TILE)
    return pl.pallas_call(
        body,
        grid_spec=pltpu.PrefetchScalarGridSpec(
            num_scalar_prefetch=1,
            grid=(2, R, plan.cap_r),
            in_specs=[pl.BlockSpec((1, 1, slots, TILE, TILE), in_map)],
            out_specs=pl.BlockSpec(
                (1, 2, R, 1, 1, plan.cap_l, TILE, TILE), lambda i, r, t, tab: (r, 0, 0, i, t, 0, 0, 0)
            ),
        ),
        out_shape=jax.ShapeDtypeStruct(shape, jnp.bfloat16),
        compiler_params=pltpu.CompilerParams(vmem_limit_bytes=VMEM_LIMIT),
        name="pack_near",
    )(table, updates)


def pack_far(plan, table, updates):
    R, L = plan.R, plan.L
    slots = updates.shape[2]
    shape = jax.ShapeDtypeStruct((R, R, 2, 2, plan.cap_r, plan.cap_l, TILE, TILE), jnp.bfloat16)
    in_block = (1, 1, slots, TILE, TILE)

    def direct(tab, x_ref, out):
        i = pl.program_id(0)
        kap = tab[plan.kap]
        h = kap // R
        for k in range(R):
            for t in range(plan.cap_l):
                b = plan.shift_entry(tab, i, lax.rem(kap + h * R + k, L), t)

                @pl.when(b >= 0)
                def _(k=k, t=t, b=b):
                    out[0, k, 0, 0, 0, t] = x_ref[0, 0, b]

    def direct_map(i, r, t, tab):
        rho, h, _ = plan.place(tab)
        return (i, 2 * jnp.maximum(plan.class_entry(tab, i, lax.rem(r + rho, R), t), 0) + 1 - h, 0, 0, 0)

    def row_group(tab, i, k, t):
        return plan.shift_entry(tab, i, lax.rem(k + tab[plan.rho] + R, L), t)

    def turned(tab, x_ref, held, out):
        i = pl.program_id(0)
        _, _, kl = plan.place(tab)

        @pl.when(row_group(tab, i, pl.program_id(1), pl.program_id(2)) >= 0)
        def _():
            for r in range(R):
                for t in range(plan.cap_r):
                    a = plan.class_entry(tab, i, lax.rem(r + kl, R), t)

                    @pl.when(a >= 0)
                    def _(r=r, t=t, a=a):
                        out[r, 0, 0, 0, t, 0] = x_ref[0, 0, a].T

    def turned_map(i, k, t, tab):
        _, h, _ = plan.place(tab)
        return (i, 2 * jnp.maximum(row_group(tab, i, k, t), 0) + 1 - h, 0, 0, 0)

    partial = pl.pallas_call(
        direct,
        grid_spec=pltpu.PrefetchScalarGridSpec(
            num_scalar_prefetch=1,
            grid=(2, R, plan.cap_r),
            in_specs=[pl.BlockSpec(in_block, direct_map)],
            out_specs=pl.BlockSpec(
                (1, R, 1, 1, 1, plan.cap_l, TILE, TILE), lambda i, r, t, tab: (r, 0, i, 0, t, 0, 0, 0)
            ),
        ),
        out_shape=shape,
        compiler_params=pltpu.CompilerParams(vmem_limit_bytes=VMEM_LIMIT),
        name="pack_far_direct",
    )(table, updates)
    return pl.pallas_call(
        turned,
        grid_spec=pltpu.PrefetchScalarGridSpec(
            num_scalar_prefetch=1,
            grid=(2, R, plan.cap_l),
            in_specs=[pl.BlockSpec(in_block, turned_map), pl.BlockSpec(memory_space=pl.ANY)],
            out_specs=pl.BlockSpec(
                (R, 1, 1, 1, plan.cap_r, 1, TILE, TILE), lambda i, k, t, tab: (0, k, i, 1, 0, t, 0, 0)
            ),
        ),
        out_shape=shape,
        input_output_aliases={2: 0},
        compiler_params=pltpu.CompilerParams(vmem_limit_bytes=VMEM_LIMIT),
        name="pack_far_turned",
    )(table, updates, partial)


def pack_panel(plan, table, updates):
    R, L = plan.R, plan.L
    slots = updates.shape[2]

    def which(tab, i):
        rho, _, _ = plan.place(tab)
        a = tab[plan.first + i]
        s = plan.get_shift(tab, i, jnp.maximum(a, 0))
        low = modr(s - rho, L) < PT
        high = modr(s - rho - R, L) < PT
        return a, low, high

    def body(tab, x_ref, out):
        i = pl.program_id(0)
        a, low, high = which(tab, i)
        there = (a >= 0) & (low | high)

        for k in range(L):
            for t in range(plan.cap_l):
                b = plan.shift_entry(tab, i, lax.rem(tab[plan.kap] + k, L), t)

                @pl.when((b >= 0) & there)
                def _(k=k, t=t, b=b):
                    out[k, 0, t] = x_ref[0, 0, b]

    def in_map(i, tab):
        a, _, high = which(tab, i)
        return (i, 2 * jnp.maximum(a, 0) + high.astype(jnp.int32), 0, 0, 0)

    return pl.pallas_call(
        body,
        grid_spec=pltpu.PrefetchScalarGridSpec(
            num_scalar_prefetch=1,
            grid=(2,),
            in_specs=[pl.BlockSpec((1, 1, slots, TILE, TILE), in_map)],
            out_specs=pl.BlockSpec((L, 1, plan.cap_l, TILE, TILE), lambda i, tab: (0, i, 0, 0, 0)),
        ),
        out_shape=jax.ShapeDtypeStruct((L, 2, plan.cap_l, TILE, TILE), jnp.bfloat16),
        compiler_params=pltpu.CompilerParams(vmem_limit_bytes=VMEM_LIMIT),
        name="pack_panel",
    )(table, updates)


def assemble_panel(plan, table, front_rows, child_rows, slots):
    R, L = plan.R, plan.L

    def body(tab, f_ref, c0_ref, c1_ref, out):
        f = pl.program_id(0)
        for cs in range(slots):
            out[cs] = f_ref[0, pl.ds(cs, TILE, stride=slots), :]
        for i, c_ref in ((0, c0_ref), (1, c1_ref)):

            @pl.when(tab[plan.first + i] >= 0)
            def _(i=i, c_ref=c_ref):
                for k in range(L):
                    for t in range(plan.cap_l):
                        b = plan.shift_entry(tab, i, lax.rem(tab[plan.kap] + k, L), t)

                        @pl.when(b >= 0)
                        def _(k=k, t=t, b=b):
                            cs = plan.get_home(tab, i, b)
                            out[cs] = out[cs] + c_ref[0, k, 0, t].astype(jnp.float32)

    def child_map(i):
        def at(f, tab):
            s = plan.get_shift(tab, i, jnp.maximum(tab[plan.first + i], 0))
            return (lax.rem(modr(s - f, L), R), 0, i, 0, 0, 0)

        return at

    child_block = (1, L, 1, plan.cap_l, TILE, TILE)
    return pl.pallas_call(
        body,
        grid_spec=pltpu.PrefetchScalarGridSpec(
            num_scalar_prefetch=1,
            grid=(PT,),
            in_specs=[
                pl.BlockSpec((1, TILE * slots, TILE), lambda f, tab: (f, 0, 0)),
                pl.BlockSpec(child_block, child_map(0)),
                pl.BlockSpec(child_block, child_map(1)),
            ],
            out_specs=pl.BlockSpec((slots, TILE, TILE), lambda f, tab: (0, f, 0)),
        ),
        out_shape=jax.ShapeDtypeStruct((slots, PD, TILE), jnp.float32),
        compiler_params=pltpu.CompilerParams(vmem_limit_bytes=VMEM_LIMIT),
        name="assemble_panel",
    )(table, front_rows, child_rows, child_rows)


def split_bf16(x):
    high = x.astype(jnp.bfloat16)
    return high, (x - high.astype(jnp.float32)).astype(jnp.bfloat16)


def solve_blocks(inverse, blocks, wide):
    count = blocks.shape[0]
    pair = 2 if count % 2 == 0 else 1
    height = blocks.shape[1]

    def body(inv, x, high, low, inv_high, inv_low):
        @pl.when(pl.program_id(0) == 0)
        def _():
            inv_high[...], inv_low[...] = split_bf16(inv[...])

        xs = [split_bf16(x[q] if height == PD else decode(x[q])) for q in range(pair)]
        xh = jnp.concatenate([p[0] for p in xs], axis=1)
        xl = jnp.concatenate([p[1] for p in xs], axis=1)
        y = jnp.dot(inv_high[...], xh, preferred_element_type=jnp.float32)
        y += jnp.dot(inv_high[...], xl, preferred_element_type=jnp.float32)
        y += jnp.dot(inv_low[...], xh, preferred_element_type=jnp.float32)
        hi, lo = split_bf16(y)
        if wide:
            high[...], low[...] = hi, lo
        else:
            for q in range(pair):
                high[q], low[q] = hi[:, q * TILE : (q + 1) * TILE], lo[:, q * TILE : (q + 1) * TILE]

    if wide:
        shape, spec = (PD, count * TILE), pl.BlockSpec((PD, pair * TILE), lambda s: (0, s))
    else:
        shape, spec = (count, PD, TILE), pl.BlockSpec((pair, PD, TILE), lambda s: (s, 0, 0))
    whole = pl.BlockSpec((PD, PD), lambda s: (0, 0))
    return pl.pallas_call(
        body,
        grid=(count // pair,),
        in_specs=[whole, pl.BlockSpec((pair, height, TILE), lambda s: (s, 0, 0))],
        out_specs=[spec, spec],
        out_shape=[jax.ShapeDtypeStruct(shape, jnp.bfloat16)] * 2,
        scratch_shapes=[pltpu.VMEM((PD, PD), jnp.bfloat16)] * 2,
        compiler_params=pltpu.CompilerParams(vmem_limit_bytes=VMEM_LIMIT),
        name="solve_blocks",
    )(inverse, blocks)


def slab_source(plan, tab, i, fr):
    a = tab[plan.at_home + i * plan.homes + fr // 2]
    lane = modr(plan.get_shift(tab, i, jnp.maximum(a, 0)) - tab[plan.rho] - plan.R * lax.rem(fr, 2), plan.L)
    return a, lax.rem(lane, plan.R), lane // plan.R


def add_blocks(plan, tab, i, fr, half, out, block, slots):
    R, L = plan.R, plan.L
    kap = tab[plan.kap]
    for k in range(R):
        for t in range(plan.cap_l):
            b = plan.shift_entry(tab, i, lax.rem(kap + half * R + k, L), t)
            cs = plan.get_home(tab, i, jnp.maximum(b, 0))

            @pl.when((b >= 0) & jnp.logical_not((cs == 0) & (kap < PT)))
            def _(k=k, t=t, cs=cs):
                at = pl.ds(cs, TILE, stride=slots)
                out[at, :] = out[at, :] + block(k, t).astype(jnp.float32)


def far_specs(plan, i):
    def direct(fr, tab):
        a, low, _ = slab_source(plan, tab, i, fr)
        return (low, 0, i, 0, tab[plan.rank + i * plan.G + jnp.maximum(a, 0)], 0, 0, 0)

    def turned(fr, tab):
        a, low, _ = slab_source(plan, tab, i, fr)
        return (0, low, i, 1, tab[plan.rank + i * plan.G + jnp.maximum(a, 0)], 0, 0, 0)

    return [
        pl.BlockSpec((1, plan.R, 1, 1, 1, plan.cap_l, TILE, TILE), direct),
        pl.BlockSpec((plan.R, 1, 1, 1, 1, plan.cap_l, TILE, TILE), turned),
    ]


def trailing(plan, table, front, factor, row_parts, col_parts, far, slots):
    R, L = plan.R, plan.L
    count = front.shape[0]
    share = slots // R

    def body(tab, f_ref, l_ref, rh, rl, ch, cl, direct0, turned0, direct1, turned1, out):
        fr = pl.program_id(0)
        rho, kap = tab[plan.rho], tab[plan.kap]
        head = (fr == 0) & (rho < PT)
        contract = (((0,), (0,)), ((), ()))
        step = 256 if slots % 2 == 0 else 128

        @pl.when(jnp.logical_not(head))
        def _():
            xh, xl = rh[0], rl[0]
            for w in range(slots * TILE // step):
                cols = pl.ds(w * step, step)
                y = lax.dot_general(xh, ch[:, cols], contract, preferred_element_type=jnp.float32)
                y += lax.dot_general(xh, cl[:, cols], contract, preferred_element_type=jnp.float32)
                y += lax.dot_general(xl, ch[:, cols], contract, preferred_element_type=jnp.float32)
                for q in range(step // TILE):
                    at = pl.ds(w * (step // TILE) + q, TILE, stride=slots)
                    out[0, at, :] = f_ref[0, at, :] - y[:, q * TILE : (q + 1) * TILE]

        h = kap // R
        for i, direct, turned in ((0, direct0, turned0), (1, direct1, turned1)):
            a, _, half = slab_source(plan, tab, i, fr)

            @pl.when((a >= 0) & jnp.logical_not(head) & (half != h))
            def _(i=i, direct=direct):
                add_blocks(plan, tab, i, fr, h, out.at[0], lambda k, t: direct[0, k, 0, 0, 0, t], slots)

            @pl.when((a >= 0) & jnp.logical_not(head) & (half == h))
            def _(i=i, turned=turned):
                add_blocks(plan, tab, i, fr, 1 - h, out.at[0], lambda k, t: turned[k, 0, 0, 0, 0, t], slots)

        @pl.when(head)
        def _():
            out[...] = jnp.zeros_like(out)

        @pl.when((kap < PT) & head)
        def _():
            out[0, pl.ds(0, TILE, stride=slots), :] = l_ref[...]

        @pl.when((kap < PT) & jnp.logical_not(head))
        def _():
            rows = pl.ds(pl.multiple_of(kap * TILE, TILE), TILE)
            x = rh[0, rows, :].astype(jnp.float32) + rl[0, rows, :].astype(jnp.float32)
            out[0, pl.ds(0, TILE, stride=slots), :] = x.T

    slab = pl.BlockSpec((1, TILE * slots, TILE), lambda fr, tab: (fr, 0, 0))

    def row_at(fr, tab):
        cs = fr // 2
        other = (lax.rem(fr, 2) != tab[plan.kap] // R).astype(jnp.int32)
        return ((cs // share * 2 + other) * share + lax.rem(cs, share), 0, 0)

    row_spec = pl.BlockSpec((1, PD, TILE), row_at)
    col_spec = pl.BlockSpec((PD, slots * TILE), lambda fr, tab: (0, 0))
    factor_spec = pl.BlockSpec(
        (TILE, TILE), lambda fr, tab: (jnp.minimum(tab[plan.rho], PT - 1), jnp.minimum(tab[plan.kap], PT - 1))
    )
    flops = 6 * count * TILE * PD * slots * TILE
    return pl.pallas_call(
        body,
        grid_spec=pltpu.PrefetchScalarGridSpec(
            num_scalar_prefetch=1,
            grid=(count,),
            in_specs=[slab, factor_spec, row_spec, row_spec, col_spec, col_spec] + far_specs(plan, 0) + far_specs(plan, 1),
            out_specs=slab,
        ),
        out_shape=jax.ShapeDtypeStruct(front.shape, jnp.float32),
        compiler_params=pltpu.CompilerParams(vmem_limit_bytes=VMEM_LIMIT),
        cost_estimate=pl.CostEstimate(flops=flops, bytes_accessed=2 * front.size * 4, transcendentals=0),
        name="trailing",
    )(table, front, factor, *row_parts, *col_parts, far, far, far, far)


def add_near(plan, table, total, near, slots):
    R = plan.R
    count, rows = total.shape[0], TILE * slots
    part = rows // STREAMS

    def body(tab, t_hbm, near_hbm, out_hbm, slab, blocks, load_sem, near_sem, store_sem):
        def loads(s, slot):
            copies = []
            for c in range(STREAMS):
                at = pl.ds(c * part, part)
                copies.append(
                    pltpu.make_async_copy(t_hbm.at[s, at], slab.at[slot, at], load_sem.at[slot, c])
                )
            for i in range(2):
                a, low, half = slab_source(plan, tab, i, s)
                rank = tab[plan.rank + i * plan.G + jnp.maximum(a, 0)]
                copies.append(
                    pltpu.make_async_copy(
                        near_hbm.at[low, half, :, i, rank], blocks.at[slot, i], near_sem.at[slot, i]
                    )
                )
            return copies

        def stores(s, slot):
            copies = []
            for c in range(STREAMS):
                at = pl.ds(c * part, part)
                copies.append(
                    pltpu.make_async_copy(slab.at[slot, at], out_hbm.at[s, at], store_sem.at[slot, c])
                )
            return copies

        def start(copies):
            for copy in copies:
                copy.start()

        def wait(copies):
            for copy in copies:
                copy.wait()

        start(loads(0, 0))
        start(loads(1, 1))

        def step(s, carry):
            slot = lax.rem(s, 4)
            ahead = lax.rem(s + 2, 4)

            @pl.when(s + 2 < count)
            def _():
                @pl.when(s >= 2)
                def _():
                    wait(stores(s - 2, ahead))

                start(loads(s + 2, ahead))

            wait(loads(s, slot))
            live = jnp.logical_not((s == 0) & (tab[plan.rho] < PT))
            for i in range(2):
                a, _, half = slab_source(plan, tab, i, s)

                @pl.when(live & (a >= 0))
                def _(i=i, half=half):
                    add_blocks(
                        plan, tab, i, s, half, slab.at[slot], lambda k, t: blocks[slot, i, k, t], slots
                    )

            start(stores(s, slot))
            return carry

        lax.fori_loop(0, count, step, 0)
        for s in range(count - 4, count):
            wait(stores(s, s % 4))

    hbm = pl.BlockSpec(memory_space=pl.ANY)
    return pl.pallas_call(
        body,
        grid_spec=pltpu.PrefetchScalarGridSpec(
            num_scalar_prefetch=1,
            grid=(1,),
            in_specs=[hbm, hbm],
            out_specs=hbm,
            scratch_shapes=[
                pltpu.VMEM((4, rows, TILE), jnp.float32),
                pltpu.VMEM((4, 2, R, plan.cap_l, TILE, TILE), jnp.bfloat16),
                pltpu.SemaphoreType.DMA((4, STREAMS)),
                pltpu.SemaphoreType.DMA((4, 2)),
                pltpu.SemaphoreType.DMA((4, STREAMS)),
            ],
        ),
        out_shape=jax.ShapeDtypeStruct(total.shape, jnp.float32),
        input_output_aliases={1: 0},
        compiler_params=pltpu.CompilerParams(vmem_limit_bytes=VMEM_LIMIT),
        name="add_near",
    )(table, total, near)


def permute(x, plan, target):
    R, L = plan.R, plan.L
    pairs = []
    for rho in range(R):
        for h in range(2):
            for kl in range(R):
                r2, h2, k2 = target(rho, h, kl)
                pairs.append((rho * L + h * R + kl, (r2 % R) * L + h2 * R + k2 % R))
    return lax.ppermute(x, AXES, pairs)


def panel_factor(diagonal):
    factor = jnp.linalg.cholesky(diagonal)
    inverse = lax.linalg.triangular_solve(
        factor, jnp.eye(PD, dtype=jnp.float32), left_side=True, lower=True
    )
    return factor, inverse


def encode(blocks):
    largest = jnp.max(jnp.abs(blocks), axis=1, keepdims=True)
    exponent = jnp.clip(jnp.ceil(jnp.log2(jnp.maximum(largest, 1e-30))), -100.0, 100.0)
    fixed = jnp.clip(jnp.round(blocks * jnp.exp2(15.0 - exponent)), -32767.0, 32767.0).astype(jnp.int32)
    words = (fixed[:, : PD // 2] << 16) | (fixed[:, PD // 2 :] & 0xFFFF)
    tail = jnp.broadcast_to(exponent.astype(jnp.int32), (blocks.shape[0], 8, TILE))
    return jnp.concatenate([words, tail], axis=1)


def decode(words):
    scale = jnp.exp2((words[PD // 2 : PD // 2 + 1] - 15).astype(jnp.float32))
    pairs = words[: PD // 2]
    fixed = jnp.concatenate([pairs >> 16, (pairs << 16) >> 16], axis=0)
    return fixed.astype(jnp.float32) * scale


def on_device(front_blocks, child_updates, child_map):
    R, L = lax.axis_size("row"), lax.axis_size(COL)
    front_rows, tile, slots, _ = front_blocks.shape
    plan = Plan(R, L, child_map.shape[1] // L, slots)
    table = make_table(plan, child_map)
    front = front_blocks.reshape(front_rows, tile * slots, tile)
    updates = jnp.transpose(child_updates, (0, 1, 3, 2, 4))

    head = pack_panel(plan, table, updates)
    table, first = lax.optimization_barrier((table, front[0]))
    front_head = lax.all_gather(first, "row")
    moved = lax.all_to_all(head, COL, 0, 0, tiled=True)

    def exchange(blocks, axes, count, after):
        flat, _ = lax.optimization_barrier((blocks.reshape((count, -1, TILE, TILE)), after))
        return lax.all_to_all(flat, axes, 0, 0, tiled=True).reshape(blocks.shape)

    far = pack_far(plan, table, updates)
    far_in = exchange(far, ("row", "lane"), R * R, (moved, front_head))

    child_head = lax.all_gather(moved, "row")
    near = pack_near(plan, table, updates)
    child_head, near = lax.optimization_barrier((child_head, near))
    panel = assemble_panel(plan, table, front_head, child_head, slots)
    diag_tiles = lax.all_gather(panel[0], COL)
    count = slots // R
    piece = encode(lax.dynamic_slice_in_dim(panel, lax.axis_index("row") * count, count, axis=0))
    piece = jnp.concatenate(
        [
            permute(piece, plan, lambda rho, h, kl: (kl, h, rho)),
            permute(piece, plan, lambda rho, h, kl: (kl, 1 - h, rho)),
        ]
    )
    diagonal = jnp.concatenate([diag_tiles[k] for k in range(PT)], axis=1)
    diagonal, piece = lax.optimization_barrier((diagonal, piece))
    near_in = exchange(near, AXES, R * L, piece)
    row_panel = lax.all_gather(piece, "lane", tiled=True)

    factor, inverse = panel_factor(diagonal)
    col_parts = solve_blocks(inverse, panel, True)
    row_parts = solve_blocks(inverse, row_panel, False)
    total = trailing(plan, table, front, factor, row_parts, col_parts, far_in, slots)
    near_in, total = lax.optimization_barrier((near_in, total))
    total = add_near(plan, table, total, near_in, slots)
    return total.reshape(front_blocks.shape)


def solution(mesh):
    rows, lanes = mesh.devices.shape
    split = Mesh(mesh.devices.reshape(rows, 2, lanes // 2), AXES)
    placed = (P(None, "row", None, COL), P(None, None, "row", None, COL), P())
    return jax.shard_map(
        on_device,
        mesh=split,
        in_specs=placed,
        out_specs=P(None, "row", None, COL),
        check_vma=False,
    )
```

```python
import functools

import jax
import jax.numpy as jnp
from jax import lax
from jax.experimental import pallas as pl
from jax.experimental.pallas import tpu as pltpu
from jax.sharding import Mesh, PartitionSpec as P

PD = 512
TILE = 128
PT = PD // TILE
COL = ("half", "lane")
AXES = ("row",) + COL
VMEM_LIMIT = 48 * 1024 * 1024
STREAMS = 4


class Plan:
    def __init__(self, rows, lanes, groups, homes):
        self.R, self.L, self.G = rows, lanes, groups
        self.cap_r = -(-groups // rows)
        self.cap_l = -(-groups // lanes)
        self.shift = 0
        self.home = self.shift + 2 * groups
        self.by_class = self.home + 2 * groups
        self.by_shift = self.by_class + 2 * rows * self.cap_r
        self.first = self.by_shift + 2 * lanes * self.cap_l
        self.homes = homes
        self.at_home = self.first + 2
        self.rank = self.at_home + 2 * homes
        self.rho = self.rank + 2 * groups
        self.kap = self.rho + 1

    def get_shift(self, tab, i, a):
        return tab[self.shift + i * self.G + a]

    def get_home(self, tab, i, a):
        return tab[self.home + i * self.G + a]

    def class_entry(self, tab, i, m, t):
        return tab[self.by_class + (i * self.R + m) * self.cap_r + t]

    def shift_entry(self, tab, i, s, t):
        return tab[self.by_shift + (i * self.L + s) * self.cap_l + t]

    def place(self, tab):
        kap = tab[self.kap]
        return tab[self.rho], kap // self.R, lax.rem(kap, self.R)


def make_table(plan, child_map):
    R, L, G = plan.R, plan.L, plan.G
    lead = child_map.reshape(2, G, L)[:, :, 0]
    shift, home = lead % L, lead // L
    ids = jnp.arange(G, dtype=jnp.int32)
    before = ids[None, :] < ids[:, None]

    def inverse(keys, count, capacity):
        rank = jnp.sum((keys[:, :, None] == keys[:, None, :]) & before[None], axis=2)
        hit = (keys[:, None, None, :] == jnp.arange(count)[None, :, None, None]) & (
            rank[:, None, None, :] == jnp.arange(capacity)[None, None, :, None]
        )
        return jnp.max(jnp.where(hit, ids[None, None, None, :], -1), axis=3)

    at_home = inverse(home, plan.homes, 1)
    same = (shift % R)[:, :, None] == (shift % R)[:, None, :]
    rank = jnp.sum(same & before[None], axis=2)
    parts = [shift, home, inverse(shift % R, R, plan.cap_r), inverse(shift, L, plan.cap_l), at_home[:, 0], at_home, rank]
    here = [lax.axis_index("row"), lax.axis_index(COL)]
    return jnp.concatenate(
        [p.reshape(-1).astype(jnp.int32) for p in parts] + [h.reshape(1).astype(jnp.int32) for h in here]
    )


def modr(value, n):
    return lax.rem(value + 2 * n, n)


def pack_near(plan, table, updates):
    R, L = plan.R, plan.L
    slots = updates.shape[2]

    def body(tab, x_ref, out):
        i = pl.program_id(0)
        kap = tab[plan.kap]
        for k in range(L):
            for t in range(plan.cap_l):
                b = plan.shift_entry(tab, i, lax.rem(kap + k, L), t)

                @pl.when(b >= 0)
                def _(k=k, t=t, b=b):
                    out[0, k // R, k % R, 0, 0, t] = x_ref[0, 0, b]

    def in_map(i, r, t, tab):
        rho, h, _ = plan.place(tab)
        return (i, 2 * jnp.maximum(plan.class_entry(tab, i, lax.rem(r + rho, R), t), 0) + h, 0, 0, 0)

    shape = (R, 2, R, 2, plan.cap_r, plan.cap_l, TILE, TILE)
    return pl.pallas_call(
        body,
        grid_spec=pltpu.PrefetchScalarGridSpec(
            num_scalar_prefetch=1,
            grid=(2, R, plan.cap_r),
            in_specs=[pl.BlockSpec((1, 1, slots, TILE, TILE), in_map)],
            out_specs=pl.BlockSpec(
                (1, 2, R, 1, 1, plan.cap_l, TILE, TILE), lambda i, r, t, tab: (r, 0, 0, i, t, 0, 0, 0)
            ),
        ),
        out_shape=jax.ShapeDtypeStruct(shape, jnp.bfloat16),
        compiler_params=pltpu.CompilerParams(vmem_limit_bytes=VMEM_LIMIT),
        name="pack_near",
    )(table, updates)


def pack_far(plan, table, updates):
    R, L = plan.R, plan.L
    slots = updates.shape[2]
    shape = jax.ShapeDtypeStruct((R, R, 2, 2, plan.cap_r, plan.cap_l, TILE, TILE), jnp.bfloat16)
    in_block = (1, 1, slots, TILE, TILE)

    def direct(tab, x_ref, out):
        i = pl.program_id(0)
        kap = tab[plan.kap]
        h = kap // R
        for k in range(R):
            for t in range(plan.cap_l):
                b = plan.shift_entry(tab, i, lax.rem(kap + h * R + k, L), t)

                @pl.when(b >= 0)
                def _(k=k, t=t, b=b):
                    out[0, k, 0, 0, 0, t] = x_ref[0, 0, b]

    def direct_map(i, r, t, tab):
        rho, h, _ = plan.place(tab)
        return (i, 2 * jnp.maximum(plan.class_entry(tab, i, lax.rem(r + rho, R), t), 0) + 1 - h, 0, 0, 0)

    def row_group(tab, i, k, t):
        return plan.shift_entry(tab, i, lax.rem(k + tab[plan.rho] + R, L), t)

    def turned(tab, x_ref, held, out):
        i = pl.program_id(0)
        _, _, kl = plan.place(tab)

        @pl.when(row_group(tab, i, pl.program_id(1), pl.program_id(2)) >= 0)
        def _():
            for r in range(R):
                for t in range(plan.cap_r):
                    a = plan.class_entry(tab, i, lax.rem(r + kl, R), t)

                    @pl.when(a >= 0)
                    def _(r=r, t=t, a=a):
                        out[r, 0, 0, 0, t, 0] = x_ref[0, 0, a].T

    def turned_map(i, k, t, tab):
        _, h, _ = plan.place(tab)
        return (i, 2 * jnp.maximum(row_group(tab, i, k, t), 0) + 1 - h, 0, 0, 0)

    partial = pl.pallas_call(
        direct,
        grid_spec=pltpu.PrefetchScalarGridSpec(
            num_scalar_prefetch=1,
            grid=(2, R, plan.cap_r),
            in_specs=[pl.BlockSpec(in_block, direct_map)],
            out_specs=pl.BlockSpec(
                (1, R, 1, 1, 1, plan.cap_l, TILE, TILE), lambda i, r, t, tab: (r, 0, i, 0, t, 0, 0, 0)
            ),
        ),
        out_shape=shape,
        compiler_params=pltpu.CompilerParams(vmem_limit_bytes=VMEM_LIMIT),
        name="pack_far_direct",
    )(table, updates)
    return pl.pallas_call(
        turned,
        grid_spec=pltpu.PrefetchScalarGridSpec(
            num_scalar_prefetch=1,
            grid=(2, R, plan.cap_l),
            in_specs=[pl.BlockSpec(in_block, turned_map), pl.BlockSpec(memory_space=pl.ANY)],
            out_specs=pl.BlockSpec(
                (R, 1, 1, 1, plan.cap_r, 1, TILE, TILE), lambda i, k, t, tab: (0, k, i, 1, 0, t, 0, 0)
            ),
        ),
        out_shape=shape,
        input_output_aliases={2: 0},
        compiler_params=pltpu.CompilerParams(vmem_limit_bytes=VMEM_LIMIT),
        name="pack_far_turned",
    )(table, updates, partial)


def pack_panel(plan, table, updates):
    R, L = plan.R, plan.L
    slots = updates.shape[2]

    def which(tab, i):
        rho, _, _ = plan.place(tab)
        a = tab[plan.first + i]
        s = plan.get_shift(tab, i, jnp.maximum(a, 0))
        low = modr(s - rho, L) < PT
        high = modr(s - rho - R, L) < PT
        return a, low, high

    def body(tab, x_ref, out):
        i = pl.program_id(0)
        a, low, high = which(tab, i)
        there = (a >= 0) & (low | high)

        for k in range(L):
            for t in range(plan.cap_l):
                b = plan.shift_entry(tab, i, lax.rem(tab[plan.kap] + k, L), t)

                @pl.when((b >= 0) & there)
                def _(k=k, t=t, b=b):
                    out[k, 0, t] = x_ref[0, 0, b]

    def in_map(i, tab):
        a, _, high = which(tab, i)
        return (i, 2 * jnp.maximum(a, 0) + high.astype(jnp.int32), 0, 0, 0)

    return pl.pallas_call(
        body,
        grid_spec=pltpu.PrefetchScalarGridSpec(
            num_scalar_prefetch=1,
            grid=(2,),
            in_specs=[pl.BlockSpec((1, 1, slots, TILE, TILE), in_map)],
            out_specs=pl.BlockSpec((L, 1, plan.cap_l, TILE, TILE), lambda i, tab: (0, i, 0, 0, 0)),
        ),
        out_shape=jax.ShapeDtypeStruct((L, 2, plan.cap_l, TILE, TILE), jnp.bfloat16),
        compiler_params=pltpu.CompilerParams(vmem_limit_bytes=VMEM_LIMIT),
        name="pack_panel",
    )(table, updates)


def assemble_panel(plan, table, front_rows, child_rows, slots):
    R, L = plan.R, plan.L

    def body(tab, f_ref, c0_ref, c1_ref, out):
        f = pl.program_id(0)
        for cs in range(slots):
            out[cs] = f_ref[0, pl.ds(cs, TILE, stride=slots), :]
        for i, c_ref in ((0, c0_ref), (1, c1_ref)):

            @pl.when(tab[plan.first + i] >= 0)
            def _(i=i, c_ref=c_ref):
                for k in range(L):
                    for t in range(plan.cap_l):
                        b = plan.shift_entry(tab, i, lax.rem(tab[plan.kap] + k, L), t)

                        @pl.when(b >= 0)
                        def _(k=k, t=t, b=b):
                            cs = plan.get_home(tab, i, b)
                            out[cs] = out[cs] + c_ref[0, k, 0, t].astype(jnp.float32)

    def child_map(i):
        def at(f, tab):
            s = plan.get_shift(tab, i, jnp.maximum(tab[plan.first + i], 0))
            return (lax.rem(modr(s - f, L), R), 0, i, 0, 0, 0)

        return at

    child_block = (1, L, 1, plan.cap_l, TILE, TILE)
    return pl.pallas_call(
        body,
        grid_spec=pltpu.PrefetchScalarGridSpec(
            num_scalar_prefetch=1,
            grid=(PT,),
            in_specs=[
                pl.BlockSpec((1, TILE * slots, TILE), lambda f, tab: (f, 0, 0)),
                pl.BlockSpec(child_block, child_map(0)),
                pl.BlockSpec(child_block, child_map(1)),
            ],
            out_specs=pl.BlockSpec((slots, TILE, TILE), lambda f, tab: (0, f, 0)),
        ),
        out_shape=jax.ShapeDtypeStruct((slots, PD, TILE), jnp.float32),
        compiler_params=pltpu.CompilerParams(vmem_limit_bytes=VMEM_LIMIT),
        name="assemble_panel",
    )(table, front_rows, child_rows, child_rows)


def split_bf16(x):
    high = x.astype(jnp.bfloat16)
    return high, (x - high.astype(jnp.float32)).astype(jnp.bfloat16)


def solve_blocks(inverse, blocks, wide):
    count = blocks.shape[0]
    pair = 2 if count % 2 == 0 else 1
    height = blocks.shape[1]

    def body(inv, x, high, low, inv_high, inv_low):
        @pl.when(pl.program_id(0) == 0)
        def _():
            inv_high[...], inv_low[...] = split_bf16(inv[...])

        xs = [split_bf16(x[q] if height == PD else decode(x[q])) for q in range(pair)]
        xh = jnp.concatenate([p[0] for p in xs], axis=1)
        xl = jnp.concatenate([p[1] for p in xs], axis=1)
        y = jnp.dot(inv_high[...], xh, preferred_element_type=jnp.float32)
        y += jnp.dot(inv_high[...], xl, preferred_element_type=jnp.float32)
        y += jnp.dot(inv_low[...], xh, preferred_element_type=jnp.float32)
        hi, lo = split_bf16(y)
        if wide:
            high[...], low[...] = hi, lo
        else:
            for q in range(pair):
                high[q], low[q] = hi[:, q * TILE : (q + 1) * TILE], lo[:, q * TILE : (q + 1) * TILE]

    if wide:
        shape, spec = (PD, count * TILE), pl.BlockSpec((PD, pair * TILE), lambda s: (0, s))
    else:
        shape, spec = (count, PD, TILE), pl.BlockSpec((pair, PD, TILE), lambda s: (s, 0, 0))
    whole = pl.BlockSpec((PD, PD), lambda s: (0, 0))
    return pl.pallas_call(
        body,
        grid=(count // pair,),
        in_specs=[whole, pl.BlockSpec((pair, height, TILE), lambda s: (s, 0, 0))],
        out_specs=[spec, spec],
        out_shape=[jax.ShapeDtypeStruct(shape, jnp.bfloat16)] * 2,
        scratch_shapes=[pltpu.VMEM((PD, PD), jnp.bfloat16)] * 2,
        compiler_params=pltpu.CompilerParams(vmem_limit_bytes=VMEM_LIMIT),
        name="solve_blocks",
    )(inverse, blocks)


def slab_source(plan, tab, i, fr):
    a = tab[plan.at_home + i * plan.homes + fr // 2]
    lane = modr(plan.get_shift(tab, i, jnp.maximum(a, 0)) - tab[plan.rho] - plan.R * lax.rem(fr, 2), plan.L)
    return a, lax.rem(lane, plan.R), lane // plan.R


def add_blocks(plan, tab, i, fr, half, out, block, slots):
    R, L = plan.R, plan.L
    kap = tab[plan.kap]
    for k in range(R):
        for t in range(plan.cap_l):
            b = plan.shift_entry(tab, i, lax.rem(kap + half * R + k, L), t)
            cs = plan.get_home(tab, i, jnp.maximum(b, 0))

            @pl.when((b >= 0) & jnp.logical_not((cs == 0) & (kap < PT)))
            def _(k=k, t=t, cs=cs):
                at = pl.ds(cs, TILE, stride=slots)
                out[at, :] = out[at, :] + block(k, t).astype(jnp.float32)


def far_specs(plan, i):
    def direct(fr, tab):
        a, low, _ = slab_source(plan, tab, i, fr)
        return (low, 0, i, 0, tab[plan.rank + i * plan.G + jnp.maximum(a, 0)], 0, 0, 0)

    def turned(fr, tab):
        a, low, _ = slab_source(plan, tab, i, fr)
        return (0, low, i, 1, tab[plan.rank + i * plan.G + jnp.maximum(a, 0)], 0, 0, 0)

    return [
        pl.BlockSpec((1, plan.R, 1, 1, 1, plan.cap_l, TILE, TILE), direct),
        pl.BlockSpec((plan.R, 1, 1, 1, 1, plan.cap_l, TILE, TILE), turned),
    ]


def trailing(plan, table, front, factor, row_parts, col_parts, far, slots):
    R, L = plan.R, plan.L
    count = front.shape[0]
    share = slots // R

    def body(tab, f_ref, l_ref, rh, rl, ch, cl, direct0, turned0, direct1, turned1, out):
        fr = pl.program_id(0)
        rho, kap = tab[plan.rho], tab[plan.kap]
        head = (fr == 0) & (rho < PT)
        contract = (((0,), (0,)), ((), ()))
        step = 256 if slots % 2 == 0 else 128

        @pl.when(jnp.logical_not(head))
        def _():
            xh, xl = rh[0], rl[0]
            for w in range(slots * TILE // step):
                cols = pl.ds(w * step, step)
                y = lax.dot_general(xh, ch[:, cols], contract, preferred_element_type=jnp.float32)
                y += lax.dot_general(xh, cl[:, cols], contract, preferred_element_type=jnp.float32)
                y += lax.dot_general(xl, ch[:, cols], contract, preferred_element_type=jnp.float32)
                for q in range(step // TILE):
                    at = pl.ds(w * (step // TILE) + q, TILE, stride=slots)
                    out[0, at, :] = f_ref[0, at, :] - y[:, q * TILE : (q + 1) * TILE]

        h = kap // R
        for i, direct, turned in ((0, direct0, turned0), (1, direct1, turned1)):
            a, _, half = slab_source(plan, tab, i, fr)

            @pl.when((a >= 0) & jnp.logical_not(head) & (half != h))
            def _(i=i, direct=direct):
                add_blocks(plan, tab, i, fr, h, out.at[0], lambda k, t: direct[0, k, 0, 0, 0, t], slots)

            @pl.when((a >= 0) & jnp.logical_not(head) & (half == h))
            def _(i=i, turned=turned):
                add_blocks(plan, tab, i, fr, 1 - h, out.at[0], lambda k, t: turned[k, 0, 0, 0, 0, t], slots)

        @pl.when(head)
        def _():
            out[...] = jnp.zeros_like(out)

        @pl.when((kap < PT) & head)
        def _():
            out[0, pl.ds(0, TILE, stride=slots), :] = l_ref[...]

        @pl.when((kap < PT) & jnp.logical_not(head))
        def _():
            rows = pl.ds(pl.multiple_of(kap * TILE, TILE), TILE)
            x = rh[0, rows, :].astype(jnp.float32) + rl[0, rows, :].astype(jnp.float32)
            out[0, pl.ds(0, TILE, stride=slots), :] = x.T

    slab = pl.BlockSpec((1, TILE * slots, TILE), lambda fr, tab: (fr, 0, 0))

    def row_at(fr, tab):
        cs = fr // 2
        other = (lax.rem(fr, 2) != tab[plan.kap] // R).astype(jnp.int32)
        return ((cs // share * 2 + other) * share + lax.rem(cs, share), 0, 0)

    row_spec = pl.BlockSpec((1, PD, TILE), row_at)
    col_spec = pl.BlockSpec((PD, slots * TILE), lambda fr, tab: (0, 0))
    factor_spec = pl.BlockSpec(
        (TILE, TILE), lambda fr, tab: (jnp.minimum(tab[plan.rho], PT - 1), jnp.minimum(tab[plan.kap], PT - 1))
    )
    flops = 6 * count * TILE * PD * slots * TILE
    return pl.pallas_call(
        body,
        grid_spec=pltpu.PrefetchScalarGridSpec(
            num_scalar_prefetch=1,
            grid=(count,),
            in_specs=[slab, factor_spec, row_spec, row_spec, col_spec, col_spec] + far_specs(plan, 0) + far_specs(plan, 1),
            out_specs=slab,
        ),
        out_shape=jax.ShapeDtypeStruct(front.shape, jnp.float32),
        compiler_params=pltpu.CompilerParams(vmem_limit_bytes=VMEM_LIMIT),
        cost_estimate=pl.CostEstimate(flops=flops, bytes_accessed=2 * front.size * 4, transcendentals=0),
        name="trailing",
    )(table, front, factor, *row_parts, *col_parts, far, far, far, far)


def add_near(plan, table, total, near, slots):
    R = plan.R
    count, rows = total.shape[0], TILE * slots
    part = rows // STREAMS

    def body(tab, t_hbm, near_hbm, out_hbm, slab, blocks, load_sem, near_sem, store_sem):
        def loads(s, slot):
            copies = []
            for c in range(STREAMS):
                at = pl.ds(c * part, part)
                copies.append(
                    pltpu.make_async_copy(t_hbm.at[s, at], slab.at[slot, at], load_sem.at[slot, c])
                )
            for i in range(2):
                a, low, half = slab_source(plan, tab, i, s)
                rank = tab[plan.rank + i * plan.G + jnp.maximum(a, 0)]
                copies.append(
                    pltpu.make_async_copy(
                        near_hbm.at[low, half, :, i, rank], blocks.at[slot, i], near_sem.at[slot, i]
                    )
                )
            return copies

        def stores(s, slot):
            copies = []
            for c in range(STREAMS):
                at = pl.ds(c * part, part)
                copies.append(
                    pltpu.make_async_copy(slab.at[slot, at], out_hbm.at[s, at], store_sem.at[slot, c])
                )
            return copies

        def start(copies):
            for copy in copies:
                copy.start()

        def wait(copies):
            for copy in copies:
                copy.wait()

        start(loads(0, 0))
        start(loads(1, 1))

        def step(s, carry):
            slot = lax.rem(s, 4)
            ahead = lax.rem(s + 2, 4)

            @pl.when(s + 2 < count)
            def _():
                @pl.when(s >= 2)
                def _():
                    wait(stores(s - 2, ahead))

                start(loads(s + 2, ahead))

            wait(loads(s, slot))
            live = jnp.logical_not((s == 0) & (tab[plan.rho] < PT))
            for i in range(2):
                a, _, half = slab_source(plan, tab, i, s)

                @pl.when(live & (a >= 0))
                def _(i=i, half=half):
                    add_blocks(
                        plan, tab, i, s, half, slab.at[slot], lambda k, t: blocks[slot, i, k, t], slots
                    )

            start(stores(s, slot))
            return carry

        lax.fori_loop(0, count, step, 0)
        for s in range(count - 4, count):
            wait(stores(s, s % 4))

    hbm = pl.BlockSpec(memory_space=pl.ANY)
    return pl.pallas_call(
        body,
        grid_spec=pltpu.PrefetchScalarGridSpec(
            num_scalar_prefetch=1,
            grid=(1,),
            in_specs=[hbm, hbm],
            out_specs=hbm,
            scratch_shapes=[
                pltpu.VMEM((4, rows, TILE), jnp.float32),
                pltpu.VMEM((4, 2, R, plan.cap_l, TILE, TILE), jnp.bfloat16),
                pltpu.SemaphoreType.DMA((4, STREAMS)),
                pltpu.SemaphoreType.DMA((4, 2)),
                pltpu.SemaphoreType.DMA((4, STREAMS)),
            ],
        ),
        out_shape=jax.ShapeDtypeStruct(total.shape, jnp.float32),
        input_output_aliases={1: 0},
        compiler_params=pltpu.CompilerParams(vmem_limit_bytes=VMEM_LIMIT),
        name="add_near",
    )(table, total, near)


def permute(x, plan, target):
    R, L = plan.R, plan.L
    pairs = []
    for rho in range(R):
        for h in range(2):
            for kl in range(R):
                r2, h2, k2 = target(rho, h, kl)
                pairs.append((rho * L + h * R + kl, (r2 % R) * L + h2 * R + k2 % R))
    return lax.ppermute(x, AXES, pairs)


def panel_factor(diagonal):
    factor = jnp.linalg.cholesky(diagonal)
    inverse = lax.linalg.triangular_solve(
        factor, jnp.eye(PD, dtype=jnp.float32), left_side=True, lower=True
    )
    return factor, inverse


def encode(blocks):
    largest = jnp.max(jnp.abs(blocks), axis=1, keepdims=True)
    exponent = jnp.clip(jnp.ceil(jnp.log2(jnp.maximum(largest, 1e-30))), -100.0, 100.0)
    fixed = jnp.clip(jnp.round(blocks * jnp.exp2(15.0 - exponent)), -32767.0, 32767.0).astype(jnp.int32)
    words = (fixed[:, : PD // 2] << 16) | (fixed[:, PD // 2 :] & 0xFFFF)
    tail = jnp.broadcast_to(exponent.astype(jnp.int32), (blocks.shape[0], 8, TILE))
    return jnp.concatenate([words, tail], axis=1)


def decode(words):
    scale = jnp.exp2((words[PD // 2 : PD // 2 + 1] - 15).astype(jnp.float32))
    pairs = words[: PD // 2]
    fixed = jnp.concatenate([pairs >> 16, (pairs << 16) >> 16], axis=0)
    return fixed.astype(jnp.float32) * scale


def on_device(front_blocks, child_updates, child_map):
    R, L = lax.axis_size("row"), lax.axis_size(COL)
    front_rows, tile, slots, _ = front_blocks.shape
    plan = Plan(R, L, child_map.shape[1] // L, slots)
    table = make_table(plan, child_map)
    front = front_blocks.reshape(front_rows, tile * slots, tile)
    updates = jnp.transpose(child_updates, (0, 1, 3, 2, 4))

    head = pack_panel(plan, table, updates)
    table, first = lax.optimization_barrier((table, front[0]))
    front_head = lax.all_gather(first, "row")
    moved = lax.all_to_all(head, COL, 0, 0, tiled=True)

    def exchange(blocks, axes, count, after):
        flat, _ = lax.optimization_barrier((blocks.reshape((count, -1, TILE, TILE)), after))
        return lax.all_to_all(flat, axes, 0, 0, tiled=True).reshape(blocks.shape)

    far = pack_far(plan, table, updates)
    far_in = exchange(far, ("row", "lane"), R * R, (moved, front_head))

    child_head = lax.all_gather(moved, "row")
    near = pack_near(plan, table, updates)
    child_head, near = lax.optimization_barrier((child_head, near))
    panel = assemble_panel(plan, table, front_head, child_head, slots)
    first_tiles = permute(panel[0], plan, lambda rho, h, kl: (rho, 1 - h, kl))
    first_tiles = jnp.where(lax.axis_index("half") == 0, panel[0], first_tiles)
    diag_tiles = lax.all_gather(first_tiles, "lane")
    count = slots // R
    piece = encode(lax.dynamic_slice_in_dim(panel, lax.axis_index("row") * count, count, axis=0))
    piece = jnp.concatenate(
        [
            permute(piece, plan, lambda rho, h, kl: (kl, h, rho)),
            permute(piece, plan, lambda rho, h, kl: (kl, 1 - h, rho)),
        ]
    )
    diagonal = jnp.concatenate([diag_tiles[k] for k in range(PT)], axis=1)
    diagonal, piece = lax.optimization_barrier((diagonal, piece))
    near_in = exchange(near, AXES, R * L, piece)
    row_panel = lax.all_gather(piece, "lane", tiled=True)

    factor, inverse = panel_factor(diagonal)
    col_parts = solve_blocks(inverse, panel, True)
    row_parts = solve_blocks(inverse, row_panel, False)
    total = trailing(plan, table, front, factor, row_parts, col_parts, far_in, slots)
    near_in, total = lax.optimization_barrier((near_in, total))
    total = add_near(plan, table, total, near_in, slots)
    return total.reshape(front_blocks.shape)


def solution(mesh):
    rows, lanes = mesh.devices.shape
    split = Mesh(mesh.devices.reshape(rows, 2, lanes // 2), AXES)
    placed = (P(None, "row", None, COL), P(None, None, "row", None, COL), P())
    return jax.shard_map(
        on_device,
        mesh=split,
        in_specs=placed,
        out_specs=P(None, "row", None, COL),
        check_vma=False,
    )
```
